32 devices in a mesh: mats: 2 (over y), col: 4 (over x, core), row: 4 (over z).
Axes of the slice: x: 2, y: 2, z: 4, core: 2. Of those that a mesh axis runs over, the one named last changes fastest.
Arguments:
- iterate: float32 [7168, 8192], P(('mats', 'row'), 'col'), parts along dimension 0, may hold values from -0.0390625 to 0.0390625
Outputs:
- update: float32 [7168, 8192], P(('mats', 'row'), 'col'), parts along dimension 0
The draws below stay inside these ranges and needn't reach their ends.
There are 2 independent parts, one for each index of `mats`. The reference program is written for one: setup_inputs(seed, part) draws one part's arguments, and reference() takes and returns one part's arrays. A program takes and returns all parts, laid end to end along the dimension named above; each array names one. Nothing has to cross between parts.
All inputs are finite; a program needn't handle non-finite values.
Results may differ from the reference program's by a relative error of at most 0.0043.
Values may be sent and summed in bfloat16 or wider, within the bound.
No kernel may reach another device: no remote copies, remote signals or barrier semaphores. Data moves between devices by JAX's collectives and lax.ppermute only.
A program may use at most 128 MiB of HBM per device.

```python
import math
import jax
import jax.numpy as jnp
from jax import lax

ORDER = 3584
COLS = 8192


def block_scale(stream_key, shape, cuts, low, high):
    factor_of, own = 1.0, jax.random.fold_in(stream_key, 6)
    for position, blocks in cuts:
        heights = jnp.exp(jax.random.uniform(jax.random.fold_in(own, position), (blocks,), jnp.float32, low / len(cuts), high / len(cuts)))
        factor_of = factor_of * jnp.repeat(heights, shape[position] // blocks).reshape([-1 if axis == position else 1 for axis in range(len(shape))])
    return factor_of


def normal_values(rng, shape, scale, bound, cuts=(), held_as=jnp.bfloat16):
    values = scale * jax.random.normal(rng, shape, jnp.float32)
    if cuts:
        values = values * block_scale(rng, shape, cuts, -0.22, 0.18)
    return jnp.clip(values, -bound, bound).astype(held_as)


def setup_inputs(seed: int = 0, part: int = 0) -> dict:
    key_list = jax.random.split(jax.random.key(seed), 2)
    part_keys = jax.random.split(jax.random.fold_in(key_list[1], part), 2)
    iterate = normal_values(part_keys[0], (ORDER, COLS), (1.0 / (ORDER ** 0.5 + COLS ** 0.5)), 0.0390625, ((0, 4), (1, 4)), jnp.float32)
    return {"iterate": iterate}


quint_a = 3.4445
quint_b = -4.775
quint_c = 2.0315

def reference(iterate):
    iter_bf = iterate.astype(jnp.bfloat16)
    gram = lax.dot_general(iter_bf, iter_bf, (((1,), (1,)), ((), ())), preferred_element_type=jnp.float32)
    gram_bf = gram.astype(jnp.bfloat16)
    first = jnp.dot(gram_bf, iter_bf, preferred_element_type=jnp.float32)
    first_bf = first.astype(jnp.bfloat16)
    second = jnp.dot(gram_bf, first_bf, preferred_element_type=jnp.float32)
    factor = 0.2 * math.sqrt(max(ORDER, COLS))
    return factor * (quint_a * iterate + quint_b * first + quint_c * second)
```

```python
import functools
import math

import jax
import jax.numpy as jnp
from jax import lax
from jax.experimental import pallas as pl
from jax.experimental.pallas import tpu as pltpu
from jax.sharding import PartitionSpec as P

ORDER = 3584
COLS = 8192

BF16 = jnp.bfloat16
F32 = jnp.float32

quint_a = 3.4445
quint_b = -4.775
quint_c = 2.0315

FACTOR = 0.2 * math.sqrt(max(ORDER, COLS))

BLOCK = 512
BLOCKS = ORDER // BLOCK
DIAGS = 4
UNITS = 2 * BLOCKS
QUARTER = 64
SLAB = ORDER // 4
GROUP = COLS // 16
PIECES = (128, 256, 256, 256)
HALVES = 2
WIDE = GROUP // HALVES
THIRDS = ((0, 5), (5, 10), (10, 14))
VMEM = 60 << 20


def shards_rows(iterate):
    iter_bf = iterate.astype(BF16)
    column_panel = lax.all_gather(iter_bf, "row", axis=0, tiled=True)
    gram_part = lax.psum_scatter(
        lax.dot_general(
            column_panel, iter_bf, (((1,), (1,)), ((), ())), preferred_element_type=F32
        ),
        "col",
        scatter_dimension=0,
        tiled=True,
    )
    gram_cols = lax.all_gather(gram_part.astype(BF16), "col", axis=0, tiled=True)
    first = lax.dot_general(
        gram_cols, column_panel, (((0,), (0,)), ((), ())), preferred_element_type=F32
    )
    second = lax.dot_general(
        gram_cols,
        lax.all_gather(first.astype(BF16), "row", axis=0, tiled=True),
        (((0,), (0,)), ((), ())),
        preferred_element_type=F32,
    )
    return FACTOR * (quint_a * iterate + quint_b * first + quint_c * second)


def flip(bit, by):
    return 1 - bit if by else bit


def place():
    col = lax.axis_index("col")
    row = lax.axis_index("row")
    return lax.axis_index("mats"), col // 2, col % 2, row // 2, row % 2


def slab_of(high, low, step):
    return 2 * flip(high, step >> 1) + flip(low, step & 1)


def over_x(a):
    return lax.ppermute(a, "col", [(0, 2), (1, 3), (2, 0), (3, 1)])


def over_core(a):
    return lax.ppermute(a, "col", [(0, 1), (1, 0), (2, 3), (3, 2)])


def over_y(a):
    return lax.ppermute(a, "mats", [(0, 1), (1, 0)])


def over_z(a, step=1):
    return lax.ppermute(a, "row", [(z, z ^ step) for z in range(4)])


def home(a, step):
    pairs = []
    for y in range(2):
        for z in range(4):
            part, slab = z // 2, (2 * y + z % 2) ^ step
            pairs.append((4 * y + z, 4 * part + slab))
    return lax.ppermute(a, ("mats", "row"), pairs)


def dot(a, b, dims):
    return lax.dot_general(a, b, (dims, ((), ())), preferred_element_type=F32)


def gram_kernel(*refs):
    count = 16 * len(PIECES)
    pieces = refs[:count]
    keep_a, send_a, keep_b, send_b, panel, total, arrived = refs[count:]
    y, x, core, high, low = place()
    diag = 2 * x + core
    n = 0
    for source in range(4):
        for step in range(4):
            start = slab_of(high, low, step) * SLAB
            for rows in PIECES:
                spot = pl.ds(pl.multiple_of(start, 128), rows)
                pltpu.make_async_copy(
                    pieces[n], panel.at[source, spot, :], arrived.at[source]
                ).start()
                start += rows
                n += 1

    def rows_of(i):
        return pl.ds(pl.multiple_of(i * BLOCK, BLOCK), BLOCK)

    for source in range(4):
        pltpu.make_async_copy(panel.at[source], panel.at[source], arrived.at[source]).wait()

        def block(i, carry):
            j = lax.rem(i + diag, BLOCKS)
            part = dot(panel[source, rows_of(i), :], panel[source, rows_of(j), :], ((1,), (1,)))
            if source == 0:
                total[i] = part
            else:
                total[i] += part
            if source == 3:
                for b in range(2):
                    def quarter(half, qy, qz):
                        at = half * 256 + (2 * qy + qz) * QUARTER
                        return total[i, pl.ds(pl.multiple_of(at, QUARTER), QUARTER), :]

                    keep_a[i, b] = quarter(0, y, b)
                    send_a[i, b] = quarter(0, 1 - y, b).astype(BF16)
                    keep_b[i, b] = quarter(1, b, low)
                    send_b[i, b] = quarter(1, b, 1 - low).astype(BF16)
            return carry

        lax.fori_loop(0, BLOCKS, block, 0)


def gram_call(pieces):
    shape = (BLOCKS, 2, QUARTER, BLOCK)
    return pl.pallas_call(
        gram_kernel,
        out_shape=[
            jax.ShapeDtypeStruct(shape, F32),
            jax.ShapeDtypeStruct(shape, BF16),
            jax.ShapeDtypeStruct(shape, F32),
            jax.ShapeDtypeStruct(shape, BF16),
        ],
        in_specs=[pl.BlockSpec(memory_space=pl.ANY)] * len(pieces),
        out_specs=[pl.BlockSpec(memory_space=pltpu.VMEM)] * 4,
        scratch_shapes=[
            pltpu.VMEM((4, ORDER, GROUP), BF16),
            pltpu.VMEM((BLOCKS, BLOCK, BLOCK), F32),
            pltpu.SemaphoreType.DMA((4,)),
        ],
        compiler_params=pltpu.CompilerParams(vmem_limit_bytes=VMEM),
        cost_estimate=pl.CostEstimate(
            flops=2 * BLOCKS * BLOCK * BLOCK * 2048, bytes_accessed=20 << 20, transcendentals=0
        ),
        name="gram",
    )(*pieces)


def step_kernel(keys, half, *refs):
    gram_pieces = refs[: len(keys)]
    refs = refs[len(keys):]
    iter_pieces = refs[: 4 * len(PIECES)]
    refs = refs[4 * len(PIECES):]
    outs = refs[:4]
    gram, panel, first, total, result, here, there, gone = refs[4:]
    y, x, core, high, low = place()
    for (third, rx, ry, rz, rk), piece in zip(keys, gram_pieces):
        lo, hi = THIRDS[third]
        diag = 2 * flip(x, rx) + flip(core, rk)
        quarter = 2 * flip(y, ry) + flip(low, rz)
        pltpu.make_async_copy(piece, gram.at[diag, pl.ds(lo, hi - lo), quarter], here).start()
    n = 0
    for step in range(4):
        start = slab_of(high, low, step) * SLAB
        for rows in PIECES:
            spot = pl.ds(pl.multiple_of(start, 128), rows)
            pltpu.make_async_copy(
                iter_pieces[n].at[:, pl.ds(half * WIDE, WIDE)], panel.at[spot, :], there
            ).start()
            start += rows
            n += 1
    pltpu.make_async_copy(panel, panel, there).wait()
    pltpu.make_async_copy(gram, gram, here).wait()

    def rows_of(i):
        return pl.ds(pl.multiple_of(i * BLOCK, BLOCK), BLOCK)

    def block(d, i):
        return gram[d, pl.ds(2 * i, 2)].reshape(BLOCK, BLOCK)

    def apply(source, i):
        got = dot(block(0, i), source[rows_of(i), :], ((1,), (0,)))
        for d in range(1, DIAGS):
            j = lax.rem(i + d, BLOCKS)
            got += dot(block(d, i), source[rows_of(j), :], ((1,), (0,)))
            j = lax.rem(i + BLOCKS - d, BLOCKS)
            got += dot(block(d, j), source[rows_of(j), :], ((0,), (0,)))
        return got

    def one(i, carry):
        got = apply(panel, i)
        first[rows_of(i), :] = got.astype(BF16)
        total[rows_of(i), :] = quint_b * got
        return carry

    def two(i, carry):
        got = apply(first, i)
        result[rows_of(i), :] = (total[rows_of(i), :] + quint_c * got).astype(BF16)
        return carry

    lax.fori_loop(0, BLOCKS, one, 0)
    lax.fori_loop(0, BLOCKS, two, 0)
    copies = []
    for step in range(4):
        start = slab_of(y, low, step) * SLAB
        copies.append(
            pltpu.make_async_copy(
                result.at[pl.ds(pl.multiple_of(start, 128), SLAB), :], outs[step], gone.at[step]
            )
        )
        copies[-1].start()
    for copy in copies:
        copy.wait()


def step_call(keys, gram_pieces, iter_pieces, half):
    count = len(gram_pieces) + len(iter_pieces)
    return pl.pallas_call(
        functools.partial(step_kernel, keys, half),
        out_shape=[jax.ShapeDtypeStruct((SLAB, WIDE), BF16)] * 4,
        in_specs=[pl.BlockSpec(memory_space=pl.ANY)] * count,
        out_specs=[pl.BlockSpec(memory_space=pl.ANY)] * 4,
        scratch_shapes=[
            pltpu.VMEM((DIAGS, UNITS, 4, QUARTER, BLOCK), BF16),
            pltpu.VMEM((ORDER, WIDE), BF16),
            pltpu.VMEM((ORDER, WIDE), BF16),
            pltpu.VMEM((ORDER, WIDE), F32),
            pltpu.VMEM((ORDER, WIDE), BF16),
            pltpu.SemaphoreType.DMA,
            pltpu.SemaphoreType.DMA,
            pltpu.SemaphoreType.DMA((4,)),
        ],
        compiler_params=pltpu.CompilerParams(vmem_limit_bytes=VMEM),
        cost_estimate=pl.CostEstimate(
            flops=4 * ORDER * ORDER * WIDE, bytes_accessed=20 << 20, transcendentals=0
        ),
        name="step",
    )(*gram_pieces, *iter_pieces)


def pick(a, at, size, axis):
    return lax.dynamic_slice_in_dim(a, at, size, axis)


def shards_cube(iterate):
    y, x, core, high, low = place()
    aligned = y == high

    own = [[] for _ in range(4)]
    start = 0
    for rows in PIECES:
        band = iterate[start : start + rows]
        keep = pick(band, y * 2 * GROUP, 2 * GROUP, 1).astype(BF16)
        other = over_y(pick(band, (1 - y) * 2 * GROUP, 2 * GROUP, 1).astype(BF16))
        near = jnp.where(aligned, keep, other)
        far = jnp.where(aligned, other, keep)
        for step in (2, 3, 1, 0):
            source = far if step >> 1 else near
            chunk = pick(source, flip(low, step & 1) * GROUP, GROUP, 1)
            own[step].append(over_z(chunk, step) if step else chunk)
        start += rows
    own = [piece for step in own for piece in step]

    across = [over_x(piece) for piece in own]
    keep_a, send_a, keep_b, send_b = gram_call(
        own + across + [over_core(piece) for piece in own] + [over_core(piece) for piece in across]
    )

    sum_a = keep_a + over_y(send_a)
    sum_b = keep_b + over_z(send_b)
    got_a = over_z(pick(sum_a, 1 - low, 1, 1).astype(BF16))
    got_b = over_y(pick(sum_b, 1 - y, 1, 1).astype(BF16))
    done_a = (pick(sum_a, low, 1, 1) + got_a).astype(BF16)
    done_b = (pick(sum_b, y, 1, 1) + got_b).astype(BF16)
    mine = jnp.concatenate([done_a, done_b], axis=1).reshape(UNITS, QUARTER, BLOCK)

    moves = {0: over_x, 1: over_y, 2: over_z}
    keys, gram_pieces = [], []
    for third, (lo, hi) in enumerate(THIRDS):
        held = {(0, 0, 0): mine[lo:hi]}
        for turn in range(3):
            axis = (third + turn) % 3
            for key, piece in list(held.items()):
                new = tuple(1 if n == axis else bit for n, bit in enumerate(key))
                held[new] = moves[axis](piece)
        for key, piece in held.items():
            keys += [(third, *key, 0), (third, *key, 1)]
            gram_pieces += [piece, over_core(piece)]

    out = (FACTOR * quint_a) * iterate
    for half in range(HALVES):
        slabs = step_call(keys, gram_pieces, own, half)
        for step in (2, 3, 1, 0):
            got = home(slabs[step], step)
            at = slab_of(high, low, step) * GROUP + half * WIDE
            out = lax.dynamic_update_slice_in_dim(
                out, pick(out, at, WIDE, 1) + FACTOR * got.astype(F32), at, 1
            )
    return out


def solution(mesh):
    shards = shards_cube if dict(mesh.shape) == {"mats": 2, "col": 4, "row": 4} else shards_rows
    in_specs = (P(("mats", "row"), "col"),)
    out_specs = P(("mats", "row"), "col")
    return jax.shard_map(shards, mesh=mesh, in_specs=in_specs, out_specs=out_specs, check_vma=False)
```

```python
import functools
import math

import jax
import jax.numpy as jnp
from jax import lax
from jax.experimental import pallas as pl
from jax.experimental.pallas import tpu as pltpu
from jax.sharding import PartitionSpec as P

ORDER = 3584
COLS = 8192

BF16 = jnp.bfloat16
F32 = jnp.float32

quint_a = 3.4445
quint_b = -4.775
quint_c = 2.0315

FACTOR = 0.2 * math.sqrt(max(ORDER, COLS))

BLOCK = 512
BLOCKS = ORDER // BLOCK
DIAGS = 4
MINE = DIAGS * BLOCKS // 2
THIRDS = ((0, 5), (5, 10), (10, 14))
PLACES = 8
UNIT = BLOCK // PLACES
TAIL = 16
SLAB = ORDER // 4
BAND = SLAB // BLOCKS
GROUP = COLS // 16
PIECES = (1, 2, 4)
HALVES = 2
WIDE = GROUP // HALVES
VMEM = 60 << 20


def shards_rows(iterate):
    iter_bf = iterate.astype(BF16)
    column_panel = lax.all_gather(iter_bf, "row", axis=0, tiled=True)
    gram_part = lax.psum_scatter(
        lax.dot_general(
            column_panel, iter_bf, (((1,), (1,)), ((), ())), preferred_element_type=F32
        ),
        "col",
        scatter_dimension=0,
        tiled=True,
    )
    gram_cols = lax.all_gather(gram_part.astype(BF16), "col", axis=0, tiled=True)
    first = lax.dot_general(
        gram_cols, column_panel, (((0,), (0,)), ((), ())), preferred_element_type=F32
    )
    second = lax.dot_general(
        gram_cols,
        lax.all_gather(first.astype(BF16), "row", axis=0, tiled=True),
        (((0,), (0,)), ((), ())),
        preferred_element_type=F32,
    )
    return FACTOR * (quint_a * iterate + quint_b * first + quint_c * second)


def flip(bit, by):
    return 1 - bit if by else bit


def place():
    col = lax.axis_index("col")
    row = lax.axis_index("row")
    return lax.axis_index("mats"), col // 2, col % 2, row // 2, row % 2


def slab_of(high, low, step):
    return 2 * flip(high, step >> 1) + flip(low, step & 1)


def place_of(x, y, low, by):
    return 4 * flip(x, by >> 2) + 2 * flip(y, by >> 1 & 1) + flip(low, by & 1)


def over_x(a):
    return lax.ppermute(a, "col", [(0, 2), (1, 3), (2, 0), (3, 1)])


def over_core(a):
    return lax.ppermute(a, "col", [(0, 1), (1, 0), (2, 3), (3, 2)])


def over_y(a):
    return lax.ppermute(a, "mats", [(0, 1), (1, 0)])


def over_z(a, step=1):
    return lax.ppermute(a, "row", [(z, z ^ step) for z in range(4)])


MOVES = {4: over_x, 2: over_y, 1: over_z}
ORDERS = ((4, 2, 1), (2, 1, 4), (1, 4, 2))


def home(a, step):
    pairs = []
    for y in range(2):
        for z in range(4):
            part, slab = z // 2, (2 * y + z % 2) ^ step
            pairs.append((4 * y + z, 4 * part + slab))
    return lax.ppermute(a, ("mats", "row"), pairs)


def dot(a, b, dims):
    return lax.dot_general(a, b, (dims, ((), ())), preferred_element_type=F32)


def place_of_block():
    return [(p, b) for p, blocks in enumerate(PIECES) for b in range(blocks)]


def on_diagonal(unit):
    shape = (UNIT, BLOCK)
    return lax.broadcasted_iota(jnp.int32, shape, 0) + unit * UNIT == lax.broadcasted_iota(
        jnp.int32, shape, 1
    )


def kept(third, stage):
    gone = sum(ORDERS[third][: stage + 1])
    return [by for by in range(PLACES) if not by & gone]


def sent(third, stage):
    return [by | ORDERS[third][stage] for by in kept(third, stage)]


def rows_sent(third, stage):
    lo, hi = THIRDS[third]
    return (hi - lo) * len(sent(third, stage)) * UNIT


def exchange_shapes(third, stage):
    lo, hi = THIRDS[third]
    return [
        jax.ShapeDtypeStruct((hi - lo, len(kept(third, stage)), UNIT, BLOCK), F32),
        jax.ShapeDtypeStruct((rows_sent(third, stage) + TAIL, BLOCK), BF16),
    ]


def write_sent(send, tail, e, parts, units, flag):
    left = jnp.zeros((1, BLOCK), F32)
    for n, (part, unit) in enumerate(zip(parts, units)):
        near = part.astype(BF16)
        row = (e * len(parts) + n) * UNIT
        send[pl.ds(row if isinstance(row, int) else pl.multiple_of(row, UNIT), UNIT), :] = near
        rest = jnp.where(on_diagonal(unit), part - near.astype(F32), 0.0)
        left += jnp.sum(rest, axis=0, keepdims=True)
    tail[pl.ds(e, 1), :] = left * flag


def gram_kernel(*refs):
    count = 2 * len(PIECES)
    inputs, refs = refs[:count], refs[count:]
    keeps, sends, refs = refs[0:6:2], refs[1:6:2], refs[6:]
    panel, turned, tails, arrived = refs[0], refs[1], refs[2:5], refs[5]
    y, x, core, high, low = place()
    for source in range(2):
        for i, (p, b) in enumerate(place_of_block()):
            for step in range(4):
                slab = slab_of(high, low, step)
                columns = pl.ds(source * GROUP, GROUP)
                pltpu.make_async_copy(
                    inputs[source * len(PIECES) + p].at[step, pl.ds(b * BAND, BAND), :],
                    panel.at[i, pl.ds(pl.multiple_of(slab * BAND, BAND), BAND), columns],
                    arrived.at[0],
                ).start()
                for n in range(2):
                    to_x, to_y = slab // 2, slab % 2
                    by = 4 * jnp.abs(to_x - x) + 2 * jnp.abs(to_y - y) + jnp.abs(n - low)
                    pltpu.make_async_copy(
                        inputs[source * len(PIECES) + p].at[step, pl.ds(b * BAND + n * UNIT, UNIT), :],
                        turned.at[i, pl.ds(pl.multiple_of(by * UNIT, UNIT), UNIT), columns],
                        arrived.at[1],
                    ).start()
    for tail in tails:
        tail[...] = jnp.zeros_like(tail)
    pltpu.make_async_copy(panel, panel, arrived.at[0]).wait()
    pltpu.make_async_copy(turned, turned, arrived.at[1]).wait()
    for third, (lo, hi) in enumerate(THIRDS):
        keep, send, tail = keeps[third], sends[third], tails[third]

        def block(e, carry):
            second = (e + lo >= BLOCKS).astype(jnp.int32)
            i = e + lo - BLOCKS * second
            j = lax.rem(i + 2 * core + second, BLOCKS)
            flag = jnp.logical_and(core == 0, second == 0).astype(F32)
            got = dot(turned[i], panel[j], ((1,), (1,)))
            for n, by in enumerate(kept(third, 0)):
                keep[e, n] = got[by * UNIT : (by + 1) * UNIT]
            parts = [got[by * UNIT : (by + 1) * UNIT] for by in sent(third, 0)]
            units = [place_of(x, y, low, by) for by in sent(third, 0)]
            write_sent(send, tail, e, parts, units, flag)
            return carry

        lax.fori_loop(0, hi - lo, block, 0)
        send[pl.ds(rows_sent(third, 0), TAIL), :] = tail[...].astype(BF16)


def add_kernel(stage, *refs):
    last = stage == 2
    keeps, gots = refs[0:6:2], refs[1:6:2]
    outs = refs[6:]
    y, x, core, high, low = place()
    for third, (lo, hi) in enumerate(THIRDS):
        keep, got = keeps[third], gots[third]
        held = kept(third, stage)
        left = got[pl.ds(rows_sent(third, stage), TAIL), :].astype(F32)
        if not last:
            nxt, send, tail = outs[2 * third], outs[2 * third + 1], outs[6 + third]
            tail[...] = jnp.zeros_like(tail)
        for e in range(hi - lo):
            diagonal = e + lo < BLOCKS
            sums = {}
            for n, by in enumerate(held):
                row = (e * len(held) + n) * UNIT
                here = keep[e, n] + got[row : row + UNIT, :].astype(F32)
                if diagonal:
                    unit = place_of(x, y, low, by)
                    here += jnp.where(on_diagonal(unit), left[e : e + 1, :], 0.0)
                sums[by] = here
            if last:
                outs[third][e] = sums[0].astype(BF16)
                continue
            for n, by in enumerate(kept(third, stage + 1)):
                nxt[e, n] = sums[by]
            going = sent(third, stage + 1)
            if diagonal:
                flag = (core == 0).astype(F32)
                units = [place_of(x, y, low, by) for by in going]
                write_sent(send, tail, e, [sums[by] for by in going], units, flag)
            else:
                for n, by in enumerate(going):
                    row = (e * len(going) + n) * UNIT
                    send[row : row + UNIT, :] = sums[by].astype(BF16)
        if not last:
            send[pl.ds(rows_sent(third, stage + 1), TAIL), :] = tail[...].astype(BF16)


def gram_call(inputs):
    return pl.pallas_call(
        gram_kernel,
        out_shape=[shape for third in range(3) for shape in exchange_shapes(third, 0)],
        in_specs=[pl.BlockSpec(memory_space=pl.ANY)] * len(inputs),
        out_specs=[pl.BlockSpec(memory_space=pltpu.VMEM)] * 6,
        scratch_shapes=[
            pltpu.VMEM((BLOCKS, BLOCK, 2 * GROUP), BF16),
            pltpu.VMEM((BLOCKS, BLOCK, 2 * GROUP), BF16),
        ]
        + [pltpu.VMEM((TAIL, BLOCK), F32)] * 3
        + [pltpu.SemaphoreType.DMA((2,))],
        compiler_params=pltpu.CompilerParams(vmem_limit_bytes=VMEM),
        cost_estimate=pl.CostEstimate(
            flops=2 * MINE * BLOCK * BLOCK * 2 * GROUP, bytes_accessed=24 << 20, transcendentals=0
        ),
        name="gram",
    )(*inputs)


def add_call(stage, inputs):
    if stage < 2:
        shapes = [shape for third in range(3) for shape in exchange_shapes(third, stage + 1)]
        scratch = [pltpu.VMEM((TAIL, BLOCK), F32)] * 3
    else:
        shapes = [jax.ShapeDtypeStruct((hi - lo, UNIT, BLOCK), BF16) for lo, hi in THIRDS]
        scratch = []
    return pl.pallas_call(
        functools.partial(add_kernel, stage),
        out_shape=shapes,
        in_specs=[pl.BlockSpec(memory_space=pltpu.VMEM)] * 6,
        out_specs=[pl.BlockSpec(memory_space=pltpu.VMEM)] * len(shapes),
        scratch_shapes=scratch,
        compiler_params=pltpu.CompilerParams(vmem_limit_bytes=40 << 20),
        cost_estimate=pl.CostEstimate(flops=1 << 22, bytes_accessed=16 << 20, transcendentals=0),
        name="add",
    )(*inputs)


def summed(parts):
    for stage in range(3):
        inputs = []
        for third in range(3):
            keep, send = parts[2 * third], parts[2 * third + 1]
            inputs += [keep, MOVES[ORDERS[third][stage]](send)]
        parts = add_call(stage, inputs)
    return parts


def gathered(mine):
    thirds = range(3)

    def move(stage, pieces):
        return [
            ([by ^ ORDERS[t][stage] for by in pieces[t][0]], MOVES[ORDERS[t][stage]](pieces[t][1]))
            for t in thirds
        ]

    def wave(*groups):
        return lax.optimization_barrier(groups)

    out = []

    def place_in(pieces, core):
        out.extend(((t, bys, core), piece) for t, (bys, piece) in enumerate(pieces))

    def across(pieces):
        place_in(pieces, 0)
        place_in([(bys, over_core(piece)) for bys, piece in pieces], 1)

    def merge(a, b):
        return [(p[0] + q[0], jnp.concatenate([p[1], q[1]])) for p, q in zip(a, b)]

    def unkeyed(pieces):
        return [piece for _, piece in pieces]

    def keyed(pieces, arrays):
        return [(bys, array) for (bys, _), array in zip(pieces, arrays)]

    own = [([0], piece) for piece in mine]
    pair = merge(own, move(0, own))
    pair = keyed(pair, wave(*unkeyed(pair)))
    second, third_a = move(1, pair), move(2, pair)
    across(pair)
    (got,) = wave((unkeyed(second), unkeyed(third_a), [piece for _, piece in out]))
    second, third_a = keyed(second, got[0]), keyed(third_a, got[1])
    out[:] = [(key, piece) for (key, _), piece in zip(out, got[2])]
    third_b = move(2, second)
    across(second)
    across(third_a)
    (got,) = wave((unkeyed(third_b), [piece for _, piece in out]))
    third_b = keyed(third_b, got[0])
    out[:] = [(key, piece) for (key, _), piece in zip(out, got[1])]
    across(third_b)
    return out


def step_kernel(keys, part, *refs):
    gram_pieces = refs[: len(keys)]
    refs = refs[len(keys) :]
    iter_pieces = refs[: len(PIECES)]
    outs = refs[len(PIECES) : len(PIECES) + 4]
    gram, panel, first, total, result, here, there, gone = refs[len(PIECES) + 4 :]
    y, x, core, high, low = place()
    for i, (p, b) in enumerate(place_of_block()):
        for step in range(4):
            pltpu.make_async_copy(
                iter_pieces[p].at[step, pl.ds(b * BAND, BAND), pl.ds(part * WIDE, WIDE)],
                panel.at[i, slab_of(high, low, step)],
                there,
            ).start()
    for (third, bys, other), piece in zip(keys, gram_pieces):
        lo, hi = THIRDS[third]
        for n, by in enumerate(bys):
            pltpu.make_async_copy(
                piece.at[n],
                gram.at[flip(core, other), pl.ds(lo, hi - lo), place_of(x, y, low, by)],
                here,
            ).start()
    pltpu.make_async_copy(panel, panel, there).wait()
    pltpu.make_async_copy(gram, gram, here).wait()

    def rows_of(i):
        return pl.ds(pl.multiple_of(i * BLOCK, BLOCK), BLOCK)

    def block(d, i):
        return gram[d // 2, BLOCKS * (d % 2) + i].reshape(BLOCK, BLOCK)

    def apply(source, i):
        got = dot(block(0, i), source(i), ((1,), (0,)))
        for d in range(1, DIAGS):
            j = lax.rem(i + d, BLOCKS)
            got += dot(block(d, i), source(j), ((1,), (0,)))
            j = lax.rem(i + BLOCKS - d, BLOCKS)
            got += dot(block(d, j), source(j), ((0,), (0,)))
        return got

    def iter_rows(i):
        return panel[i].reshape(BLOCK, WIDE)

    def one(i, carry):
        got = apply(iter_rows, i)
        first[rows_of(i), :] = got.astype(BF16)
        total[rows_of(i), :] = quint_a * iter_rows(i).astype(F32) + quint_b * got
        return carry

    def two(i, carry):
        got = apply(lambda j: first[rows_of(j), :], i)
        result[i] = (total[rows_of(i), :] + quint_c * got).astype(BF16).reshape(4, BAND, WIDE)
        return carry

    lax.fori_loop(0, BLOCKS, one, 0)
    lax.fori_loop(0, BLOCKS, two, 0)
    copies = []
    for step in range(4):
        copies.append(
            pltpu.make_async_copy(
                result.at[:, slab_of(y, low, step)], outs[step], gone.at[step]
            )
        )
        copies[-1].start()
    for copy in copies:
        copy.wait()


def step_call(keys, gram_pieces, iter_pieces, part):
    count = len(gram_pieces) + len(iter_pieces)
    return pl.pallas_call(
        functools.partial(step_kernel, keys, part),
        out_shape=[jax.ShapeDtypeStruct((BLOCKS, BAND, WIDE), BF16)] * 4,
        in_specs=[pl.BlockSpec(memory_space=pl.ANY)] * count,
        out_specs=[pl.BlockSpec(memory_space=pl.ANY)] * 4,
        scratch_shapes=[
            pltpu.VMEM((2, MINE, PLACES, UNIT, BLOCK), BF16),
            pltpu.VMEM((BLOCKS, 4, BAND, WIDE), BF16),
            pltpu.VMEM((ORDER, WIDE), BF16),
            pltpu.VMEM((ORDER, WIDE), F32),
            pltpu.VMEM((BLOCKS, 4, BAND, WIDE), BF16),
            pltpu.SemaphoreType.DMA,
            pltpu.SemaphoreType.DMA,
            pltpu.SemaphoreType.DMA((4,)),
        ],
        compiler_params=pltpu.CompilerParams(vmem_limit_bytes=VMEM),
        cost_estimate=pl.CostEstimate(
            flops=4 * ORDER * ORDER * WIDE, bytes_accessed=20 << 20, transcendentals=0
        ),
        name="step",
    )(*gram_pieces, *iter_pieces)


def pick(a, at, size, axis):
    return lax.dynamic_slice_in_dim(a, at, size, axis)


def panels(iterate):
    y, x, core, high, low = place()
    aligned = y == high
    starts = [sum(PIECES[:n]) * BAND for n in range(len(PIECES) + 1)]

    def cast(n, at):
        band = iterate[starts[n] : starts[n + 1]]
        return pick(band, at * 2 * GROUP, 2 * GROUP, 1).astype(BF16)

    def chunks(keep, other):
        near, far = jnp.where(aligned, keep, other), jnp.where(aligned, other, keep)
        return [
            pick(far if step >> 1 else near, flip(low, step & 1) * GROUP, GROUP, 1)
            for step in range(4)
        ]

    own, beside = [], []
    keep, other = cast(0, y), over_y(cast(0, 1 - y))
    for n in range(len(PIECES)):
        ready = chunks(keep, other)
        more = n + 1 < len(PIECES)
        ahead = [cast(n + 1, y), cast(n + 1, 1 - y)] if more else []
        ready, ahead, done = lax.optimization_barrier((ready, ahead, own[-1:]))
        got = [ready[0]] + [over_z(ready[step], step) for step in (1, 2, 3)]
        if more:
            keep, other = ahead[0], over_y(ahead[1])
        beside += [over_core(piece) for piece in done]
        own.append(jnp.stack(got))
    beside.append(over_core(own[-1]))
    return own, beside


def shards_cube(iterate):
    y, x, core, high, low = place()
    own, beside = panels(iterate)
    out = (FACTOR * quint_a) * (iterate - lax.reduce_precision(iterate, 8, 7))
    out, own[0] = lax.optimization_barrier((out, own[0]))
    mine = summed(gram_call(own + beside))
    entries = gathered([piece[None] for piece in mine])
    keys = [key for key, _ in entries]
    gram_pieces = [piece.reshape(-1, *piece.shape[-3:]) for _, piece in entries]

    before = None
    for part in range(HALVES):
        slabs = step_call(keys, gram_pieces, own, part)
        if before is not None:
            slabs, before = lax.optimization_barrier((slabs, before))
        got = [home(slabs[step], step) for step in range(4)]
        for step in range(4):
            at = slab_of(high, low, step) * GROUP + part * WIDE
            piece = FACTOR * got[step].reshape(SLAB, WIDE).astype(F32)
            out = lax.dynamic_update_slice_in_dim(out, pick(out, at, WIDE, 1) + piece, at, 1)
        before = got
    return out


def solution(mesh):
    shards = shards_cube if dict(mesh.shape) == {"mats": 2, "col": 4, "row": 4} else shards_rows
    in_specs = (P(("mats", "row"), "col"),)
    out_specs = P(("mats", "row"), "col")
    return jax.shard_map(shards, mesh=mesh, in_specs=in_specs, out_specs=out_specs, check_vma=False)
```

```python
import functools
import math

import jax
import jax.numpy as jnp
from jax import lax
from jax.experimental import pallas as pl
from jax.experimental.pallas import tpu as pltpu
from jax.sharding import PartitionSpec as P

ORDER = 3584
COLS = 8192

BF16 = jnp.bfloat16
F32 = jnp.float32

quint_a = 3.4445
quint_b = -4.775
quint_c = 2.0315

FACTOR = 0.2 * math.sqrt(max(ORDER, COLS))

BLOCK = 512
BLOCKS = ORDER // BLOCK
DIAGS = 4
MINE = DIAGS * BLOCKS // 2
THIRDS = ((0, 5), (5, 10), (10, 14))
PLACES = 8
UNIT = BLOCK // PLACES
TAIL = 16
SLAB = ORDER // 4
BAND = SLAB // BLOCKS
GROUP = COLS // 16
PIECES = (1, 2, 4)
HALVES = 2
WIDE = GROUP // HALVES
GRAM_VMEM = 28 << 20
STEP_VMEM = 60 << 20


def shards_rows(iterate):
    iter_bf = iterate.astype(BF16)
    column_panel = lax.all_gather(iter_bf, "row", axis=0, tiled=True)
    gram_part = lax.psum_scatter(
        lax.dot_general(
            column_panel, iter_bf, (((1,), (1,)), ((), ())), preferred_element_type=F32
        ),
        "col",
        scatter_dimension=0,
        tiled=True,
    )
    gram_cols = lax.all_gather(gram_part.astype(BF16), "col", axis=0, tiled=True)
    first = lax.dot_general(
        gram_cols, column_panel, (((0,), (0,)), ((), ())), preferred_element_type=F32
    )
    second = lax.dot_general(
        gram_cols,
        lax.all_gather(first.astype(BF16), "row", axis=0, tiled=True),
        (((0,), (0,)), ((), ())),
        preferred_element_type=F32,
    )
    return FACTOR * (quint_a * iterate + quint_b * first + quint_c * second)


def flip(bit, by):
    return 1 - bit if by else bit


def place():
    col = lax.axis_index("col")
    row = lax.axis_index("row")
    return lax.axis_index("mats"), col // 2, col % 2, row // 2, row % 2


def slab_of(high, low, step):
    return 2 * flip(high, step >> 1) + flip(low, step & 1)


def place_of(x, y, low, by):
    return 4 * flip(x, by >> 2) + 2 * flip(y, by >> 1 & 1) + flip(low, by & 1)


def over_x(a):
    return lax.ppermute(a, "col", [(0, 2), (1, 3), (2, 0), (3, 1)])


def over_core(a):
    return lax.ppermute(a, "col", [(0, 1), (1, 0), (2, 3), (3, 2)])


def over_y(a):
    return lax.ppermute(a, "mats", [(0, 1), (1, 0)])


def over_z(a, step=1):
    return lax.ppermute(a, "row", [(z, z ^ step) for z in range(4)])


MOVES = {4: over_x, 2: over_y, 1: over_z}
ORDERS = ((4, 2, 1), (2, 1, 4), (1, 4, 2))


def home(a, step):
    pairs = []
    for y in range(2):
        for z in range(4):
            part, slab = z // 2, (2 * y + z % 2) ^ step
            pairs.append((4 * y + z, 4 * part + slab))
    return lax.ppermute(a, ("mats", "row"), pairs)


def dot(a, b, dims):
    return lax.dot_general(a, b, (dims, ((), ())), preferred_element_type=F32)


def place_of_block():
    return [(p, b) for p, blocks in enumerate(PIECES) for b in range(blocks)]


def on_diagonal(unit):
    shape = (UNIT, BLOCK)
    return lax.broadcasted_iota(jnp.int32, shape, 0) + unit * UNIT == lax.broadcasted_iota(
        jnp.int32, shape, 1
    )


def kept(third, stage):
    gone = sum(ORDERS[third][: stage + 1])
    return [by for by in range(PLACES) if not by & gone]


def sent(third, stage):
    return [by | ORDERS[third][stage] for by in kept(third, stage)]


def rows_sent(third, stage):
    lo, hi = THIRDS[third]
    return (hi - lo) * len(sent(third, stage)) * UNIT


def exchange_shapes(third, stage):
    lo, hi = THIRDS[third]
    return [
        jax.ShapeDtypeStruct((hi - lo, len(kept(third, stage)), UNIT, BLOCK), F32),
        jax.ShapeDtypeStruct((rows_sent(third, stage) + TAIL, BLOCK), BF16),
    ]


def write_sent(send, tail, e, parts, units, flag):
    left = jnp.zeros((1, BLOCK), F32)
    for n, (part, unit) in enumerate(zip(parts, units)):
        near = part.astype(BF16)
        row = (e * len(parts) + n) * UNIT
        send[pl.ds(row if isinstance(row, int) else pl.multiple_of(row, UNIT), UNIT), :] = near
        rest = jnp.where(on_diagonal(unit), part - near.astype(F32), 0.0)
        left += jnp.sum(rest, axis=0, keepdims=True)
    tail[pl.ds(e, 1), :] = left * flag


def gram_kernel(*refs):
    count = 2 * len(PIECES)
    inputs, outs, refs = refs[:count], refs[count : count + 6], refs[count + 6 :]
    keeps, sends, tails = refs[0:6:2], refs[1:6:2], refs[6:9]
    panel, arrived, gone = refs[9:]
    y, x, core, high, low = place()
    for source in range(2):
        for i, (p, b) in enumerate(place_of_block()):
            for step in range(4):
                spot = pl.multiple_of(slab_of(high, low, step) * BAND, BAND)
                pltpu.make_async_copy(
                    inputs[source * len(PIECES) + p].at[step, pl.ds(b * BAND, BAND), :],
                    panel.at[i, pl.ds(spot, BAND), pl.ds(source * GROUP, GROUP)],
                    arrived,
                ).start()
    for tail in tails:
        tail[...] = jnp.zeros_like(tail)
    pltpu.make_async_copy(panel, panel, arrived).wait()
    for third, (lo, hi) in enumerate(THIRDS):
        keep, send, tail = keeps[third], sends[third], tails[third]
        size = len(sent(third, 0)) * UNIT

        def block(e, carry):
            second = (e + lo >= BLOCKS).astype(jnp.int32)
            i = e + lo - BLOCKS * second
            j = lax.rem(i + 2 * core + second, BLOCKS)
            flag = jnp.logical_and(core == 0, second == 0).astype(F32)
            rows = [
                panel[i, pl.ds(pl.multiple_of(place_of(x, y, low, by) * UNIT, UNIT), UNIT), :]
                for by in range(PLACES)
            ]
            got = dot(jnp.concatenate(rows), panel[j], ((1,), (1,)))
            for n, by in enumerate(kept(third, 0)):
                keep[e, n] = got[by * UNIT : (by + 1) * UNIT]
            parts = [got[by * UNIT : (by + 1) * UNIT] for by in sent(third, 0)]
            units = [place_of(x, y, low, by) for by in sent(third, 0)]
            write_sent(send, tail, e, parts, units, flag)
            pltpu.make_async_copy(keep.at[e], outs[2 * third].at[e], gone.at[2 * third]).start()
            rows = pl.ds(pl.multiple_of(e * size, size), size)
            pltpu.make_async_copy(
                send.at[rows, :], outs[2 * third + 1].at[rows, :], gone.at[2 * third + 1]
            ).start()
            return carry

        lax.fori_loop(0, hi - lo, block, 0)
        rows = pl.ds(rows_sent(third, 0), TAIL)
        send[rows, :] = tail[...].astype(BF16)
        pltpu.make_async_copy(
            send.at[rows, :], outs[2 * third + 1].at[rows, :], gone.at[2 * third + 1]
        ).start()
    for third in range(3):
        for n, ref in ((2 * third, keeps[third]), (2 * third + 1, sends[third])):
            pltpu.make_async_copy(ref, outs[n], gone.at[n]).wait()


def add_kernel(stage, *refs):
    last = stage == 2
    keeps, gots = refs[0:6:2], refs[1:6:2]
    outs = refs[6:]
    y, x, core, high, low = place()
    for third, (lo, hi) in enumerate(THIRDS):
        keep, got = keeps[third], gots[third]
        held = kept(third, stage)
        left = got[pl.ds(rows_sent(third, stage), TAIL), :].astype(F32)
        if not last:
            nxt, send, tail = outs[2 * third], outs[2 * third + 1], outs[6 + third]
            tail[...] = jnp.zeros_like(tail)
        for e in range(hi - lo):
            diagonal = e + lo < BLOCKS
            sums = {}
            for n, by in enumerate(held):
                row = (e * len(held) + n) * UNIT
                here = keep[e, n] + got[row : row + UNIT, :].astype(F32)
                if diagonal:
                    unit = place_of(x, y, low, by)
                    here += jnp.where(on_diagonal(unit), left[e : e + 1, :], 0.0)
                sums[by] = here
            if last:
                outs[third][e] = sums[0].astype(BF16)
                continue
            for n, by in enumerate(kept(third, stage + 1)):
                nxt[e, n] = sums[by]
            going = sent(third, stage + 1)
            if diagonal:
                flag = (core == 0).astype(F32)
                units = [place_of(x, y, low, by) for by in going]
                write_sent(send, tail, e, [sums[by] for by in going], units, flag)
            else:
                for n, by in enumerate(going):
                    row = (e * len(going) + n) * UNIT
                    send[row : row + UNIT, :] = sums[by].astype(BF16)
        if not last:
            send[pl.ds(rows_sent(third, stage + 1), TAIL), :] = tail[...].astype(BF16)


def gram_call(inputs):
    shapes = [shape for third in range(3) for shape in exchange_shapes(third, 0)]
    return pl.pallas_call(
        gram_kernel,
        out_shape=shapes,
        in_specs=[pl.BlockSpec(memory_space=pl.ANY)] * len(inputs),
        out_specs=[pl.BlockSpec(memory_space=pl.ANY)] * 6,
        scratch_shapes=[pltpu.VMEM(shape.shape, shape.dtype) for shape in shapes]
        + [pltpu.VMEM((TAIL, BLOCK), F32)] * 3
        + [
            pltpu.VMEM((BLOCKS, BLOCK, 2 * GROUP), BF16),
            pltpu.SemaphoreType.DMA,
            pltpu.SemaphoreType.DMA((6,)),
        ],
        compiler_params=pltpu.CompilerParams(vmem_limit_bytes=GRAM_VMEM),
        cost_estimate=pl.CostEstimate(
            flops=2 * MINE * BLOCK * BLOCK * 2 * GROUP, bytes_accessed=24 << 20, transcendentals=0
        ),
        name="gram",
    )(*inputs)


def add_call(stage, inputs):
    if stage < 2:
        shapes = [shape for third in range(3) for shape in exchange_shapes(third, stage + 1)]
        scratch = [pltpu.VMEM((TAIL, BLOCK), F32)] * 3
    else:
        shapes = [jax.ShapeDtypeStruct((hi - lo, UNIT, BLOCK), BF16) for lo, hi in THIRDS]
        scratch = []
    return pl.pallas_call(
        functools.partial(add_kernel, stage),
        out_shape=shapes,
        in_specs=[pl.BlockSpec(memory_space=pltpu.VMEM)] * 6,
        out_specs=[pl.BlockSpec(memory_space=pltpu.VMEM)] * len(shapes),
        scratch_shapes=scratch,
        compiler_params=pltpu.CompilerParams(vmem_limit_bytes=40 << 20),
        cost_estimate=pl.CostEstimate(flops=1 << 22, bytes_accessed=16 << 20, transcendentals=0),
        name="add",
    )(*inputs)


def summed(parts):
    for stage in range(3):
        inputs = []
        for third in range(3):
            keep, send = parts[2 * third], parts[2 * third + 1]
            inputs += [keep, MOVES[ORDERS[third][stage]](send)]
        parts = add_call(stage, inputs)
    return parts


def gathered(mine):
    thirds = range(3)

    def move(stage, pieces):
        return [
            ([by ^ ORDERS[t][stage] for by in pieces[t][0]], MOVES[ORDERS[t][stage]](pieces[t][1]))
            for t in thirds
        ]

    def wave(*groups):
        return lax.optimization_barrier(groups)

    out = []

    def place_in(pieces, core):
        out.extend(((t, bys, core), piece) for t, (bys, piece) in enumerate(pieces))

    def across(pieces):
        place_in(pieces, 0)
        place_in([(bys, over_core(piece)) for bys, piece in pieces], 1)

    def merge(a, b):
        return [(p[0] + q[0], jnp.concatenate([p[1], q[1]])) for p, q in zip(a, b)]

    def unkeyed(pieces):
        return [piece for _, piece in pieces]

    def keyed(pieces, arrays):
        return [(bys, array) for (bys, _), array in zip(pieces, arrays)]

    def ordered(*groups):
        done = wave([unkeyed(group) for group in groups], [piece for _, piece in out])
        out[:] = [(key, piece) for (key, _), piece in zip(out, done[1])]
        return [keyed(group, arrays) for group, arrays in zip(groups, done[0])]

    own = [([0], piece) for piece in mine]
    (pair,) = ordered(merge(own, move(0, own)))
    second = move(1, pair)
    across(pair)
    pair, second = ordered(pair, second)
    third_a = move(2, pair)
    across(second)
    second, third_a = ordered(second, third_a)
    third_b = move(2, second)
    across(third_a)
    (third_b,) = ordered(third_b)
    across(third_b)
    return out


def step_kernel(keys, part, *refs):
    gram_pieces = refs[: len(keys)]
    refs = refs[len(keys) :]
    iter_pieces = refs[: len(PIECES)]
    outs = refs[len(PIECES) : len(PIECES) + 4]
    gram, panel, first, total, result, here, there, gone = refs[len(PIECES) + 4 :]
    y, x, core, high, low = place()
    for i, (p, b) in enumerate(place_of_block()):
        for step in range(4):
            pltpu.make_async_copy(
                iter_pieces[p].at[step, pl.ds(b * BAND, BAND), pl.ds(part * WIDE, WIDE)],
                panel.at[i, slab_of(high, low, step)],
                there,
            ).start()
    for (third, bys, other), piece in zip(keys, gram_pieces):
        lo, hi = THIRDS[third]
        for n, by in enumerate(bys):
            pltpu.make_async_copy(
                piece.at[n],
                gram.at[flip(core, other), pl.ds(lo, hi - lo), place_of(x, y, low, by)],
                here,
            ).start()
    pltpu.make_async_copy(panel, panel, there).wait()
    pltpu.make_async_copy(gram, gram, here).wait()

    def rows_of(i):
        return pl.ds(pl.multiple_of(i * BLOCK, BLOCK), BLOCK)

    def block(d, i):
        return gram[d // 2, BLOCKS * (d % 2) + i].reshape(BLOCK, BLOCK)

    def apply(source, i):
        got = dot(block(0, i), source(i), ((1,), (0,)))
        for d in range(1, DIAGS):
            j = lax.rem(i + d, BLOCKS)
            got += dot(block(d, i), source(j), ((1,), (0,)))
            j = lax.rem(i + BLOCKS - d, BLOCKS)
            got += dot(block(d, j), source(j), ((0,), (0,)))
        return got

    def iter_rows(i):
        return panel[i].reshape(BLOCK, WIDE)

    def one(i, carry):
        got = apply(iter_rows, i)
        first[rows_of(i), :] = got.astype(BF16)
        total[rows_of(i), :] = quint_a * iter_rows(i).astype(F32) + quint_b * got
        return carry

    def two(i, carry):
        got = apply(lambda j: first[rows_of(j), :], i)
        result[i] = (total[rows_of(i), :] + quint_c * got).astype(BF16).reshape(4, BAND, WIDE)
        return carry

    lax.fori_loop(0, BLOCKS, one, 0)
    lax.fori_loop(0, BLOCKS, two, 0)
    copies = []
    for step in range(4):
        copies.append(
            pltpu.make_async_copy(
                result.at[:, slab_of(y, low, step)], outs[step], gone.at[step]
            )
        )
        copies[-1].start()
    for copy in copies:
        copy.wait()


def step_call(keys, gram_pieces, iter_pieces, part):
    count = len(gram_pieces) + len(iter_pieces)
    return pl.pallas_call(
        functools.partial(step_kernel, keys, part),
        out_shape=[jax.ShapeDtypeStruct((BLOCKS, BAND, WIDE), BF16)] * 4,
        in_specs=[pl.BlockSpec(memory_space=pl.ANY)] * count,
        out_specs=[pl.BlockSpec(memory_space=pl.ANY)] * 4,
        scratch_shapes=[
            pltpu.VMEM((2, MINE, PLACES, UNIT, BLOCK), BF16),
            pltpu.VMEM((BLOCKS, 4, BAND, WIDE), BF16),
            pltpu.VMEM((ORDER, WIDE), BF16),
            pltpu.VMEM((ORDER, WIDE), F32),
            pltpu.VMEM((BLOCKS, 4, BAND, WIDE), BF16),
            pltpu.SemaphoreType.DMA,
            pltpu.SemaphoreType.DMA,
            pltpu.SemaphoreType.DMA((4,)),
        ],
        compiler_params=pltpu.CompilerParams(vmem_limit_bytes=STEP_VMEM),
        cost_estimate=pl.CostEstimate(
            flops=4 * ORDER * ORDER * WIDE, bytes_accessed=20 << 20, transcendentals=0
        ),
        name="step",
    )(*gram_pieces, *iter_pieces)


def pick(a, at, size, axis):
    return lax.dynamic_slice_in_dim(a, at, size, axis)


def panels(iterate):
    y, x, core, high, low = place()
    aligned = y == high
    starts = [sum(PIECES[:n]) * BAND for n in range(len(PIECES) + 1)]

    def cast(n, at):
        band = iterate[starts[n] : starts[n + 1]]
        return pick(band, at * 2 * GROUP, 2 * GROUP, 1).astype(BF16)

    def chunks(keep, other):
        near, far = jnp.where(aligned, keep, other), jnp.where(aligned, other, keep)
        return [
            pick(far if step >> 1 else near, flip(low, step & 1) * GROUP, GROUP, 1)
            for step in range(4)
        ]

    own, beside = [], []
    keep, other = cast(0, y), over_y(cast(0, 1 - y))
    for n in range(len(PIECES)):
        ready = chunks(keep, other)
        more = n + 1 < len(PIECES)
        ahead = [cast(n + 1, y), cast(n + 1, 1 - y)] if more else []
        ready, ahead, done = lax.optimization_barrier((ready, ahead, own[-1:]))
        got = [ready[0]] + [over_z(ready[step], step) for step in (1, 2, 3)]
        if more:
            keep, other = ahead[0], over_y(ahead[1])
        beside += [over_core(piece) for piece in done]
        own.append(jnp.stack(got))
    beside.append(over_core(own[-1]))
    return own, beside


def shards_cube(iterate):
    y, x, core, high, low = place()
    own, beside = panels(iterate)
    out = (FACTOR * quint_a) * (iterate - lax.reduce_precision(iterate, 8, 7))
    out, own[0] = lax.optimization_barrier((out, own[0]))
    mine = summed(gram_call(own + beside))
    entries = gathered([piece[None] for piece in mine])
    keys = [key for key, _ in entries]
    gram_pieces = [piece.reshape(-1, *piece.shape[-3:]) for _, piece in entries]

    before = None
    for part in range(HALVES):
        slabs = step_call(keys, gram_pieces, own, part)
        if before is not None:
            slabs, before = lax.optimization_barrier((slabs, before))
        got = [home(slabs[step], step) for step in range(4)]
        for step in range(4):
            at = slab_of(high, low, step) * GROUP + part * WIDE
            piece = FACTOR * got[step].reshape(SLAB, WIDE).astype(F32)
            out = lax.dynamic_update_slice_in_dim(out, pick(out, at, WIDE, 1) + piece, at, 1)
        before = got
    return out


def solution(mesh):
    shards = shards_cube if dict(mesh.shape) == {"mats": 2, "col": 4, "row": 4} else shards_rows
    in_specs = (P(("mats", "row"), "col"),)
    out_specs = P(("mats", "row"), "col")
    return jax.shard_map(shards, mesh=mesh, in_specs=in_specs, out_specs=out_specs, check_vma=False)
```

```python
import functools
import math

import jax
import jax.numpy as jnp
from jax import lax
from jax.experimental import pallas as pl
from jax.experimental.pallas import tpu as pltpu
from jax.sharding import PartitionSpec as P

ORDER = 3584
COLS = 8192

BF16 = jnp.bfloat16
F32 = jnp.float32

quint_a = 3.4445
quint_b = -4.775
quint_c = 2.0315

FACTOR = 0.2 * math.sqrt(max(ORDER, COLS))

BLOCK = 512
BLOCKS = ORDER // BLOCK
DIAGS = 4
MINE = DIAGS * BLOCKS // 2
THIRDS = ((0, 5), (5, 10), (10, 14))
PLACES = 8
UNIT = BLOCK // PLACES
TAIL = 16
SLAB = ORDER // 4
BAND = SLAB // BLOCKS
GROUP = COLS // 16
HOPS = (1, 2, 4)
LAST = (1, 2, 1)
PIECES = (3, 4)
HALVES = 2
WIDE = GROUP // HALVES
GRAM_VMEM = 28 << 20
STEP_VMEM = 60 << 20


def shards_rows(iterate):
    iter_bf = iterate.astype(BF16)
    column_panel = lax.all_gather(iter_bf, "row", axis=0, tiled=True)
    gram_part = lax.psum_scatter(
        lax.dot_general(
            column_panel, iter_bf, (((1,), (1,)), ((), ())), preferred_element_type=F32
        ),
        "col",
        scatter_dimension=0,
        tiled=True,
    )
    gram_cols = lax.all_gather(gram_part.astype(BF16), "col", axis=0, tiled=True)
    first = lax.dot_general(
        gram_cols, column_panel, (((0,), (0,)), ((), ())), preferred_element_type=F32
    )
    second = lax.dot_general(
        gram_cols,
        lax.all_gather(first.astype(BF16), "row", axis=0, tiled=True),
        (((0,), (0,)), ((), ())),
        preferred_element_type=F32,
    )
    return FACTOR * (quint_a * iterate + quint_b * first + quint_c * second)


def flip(bit, by):
    return 1 - bit if by else bit


def place():
    col = lax.axis_index("col")
    row = lax.axis_index("row")
    return lax.axis_index("mats"), col // 2, col % 2, row // 2, row % 2


def slab_of(high, low, step):
    return 2 * flip(high, step >> 1) + flip(low, step & 1)


def place_of(x, y, low, by):
    return 4 * flip(x, by >> 2) + 2 * flip(y, by >> 1 & 1) + flip(low, by & 1)


def over_x(a):
    return lax.ppermute(a, "col", [(0, 2), (1, 3), (2, 0), (3, 1)])


def over_core(a):
    return lax.ppermute(a, "col", [(0, 1), (1, 0), (2, 3), (3, 2)])


def over_y(a):
    return lax.ppermute(a, "mats", [(0, 1), (1, 0)])


def over_z(a, step=1):
    return lax.ppermute(a, "row", [(z, z ^ step) for z in range(4)])


MOVES = {4: over_x, 2: over_y, 1: over_z}
ORDERS = ((4, 2, 1), (2, 1, 4), (1, 4, 2))

EARLY = (((0, 0), (1, 0), (2, 0)), ((0, 1), (1, 1), (0, 2)))
LATE = [
    (i, d) for d in range(DIAGS) for i in range(BLOCKS) if (i, d) not in EARLY[0] + EARLY[1]
]
LATE = (LATE[: MINE - 3], LATE[MINE - 3 :])
EARLY_GROUPS = tuple(
    ([core[lo:hi] for core in EARLY], order)
    for (lo, hi), order in (((0, 3), (4, 2, 1)),)
)
LATE_GROUPS = tuple(
    ([core[lo:hi] for core in LATE], order)
    for (lo, hi), order in zip(((0, 4), (4, 8), (8, 11)), ORDERS)
)
SPOT = {
    block: core * MINE + THIRDS[third][0] + n
    for core in range(2)
    for third in range(3)
    for n, block in enumerate([EARLY[core][third]] + LATE_GROUPS[third][0][core])
}


def lookup(index, values):
    got = values[0]
    for n, value in enumerate(values[1:], 1):
        got = jnp.where(index == n, value, got)
    return got


def home(a, step):
    pairs = []
    for y in range(2):
        for z in range(4):
            part, slab = z // 2, (2 * y + z % 2) ^ step
            pairs.append((4 * y + z, 4 * part + slab))
    return lax.ppermute(a, ("mats", "row"), pairs)


def dot(a, b, dims):
    return lax.dot_general(a, b, (dims, ((), ())), preferred_element_type=F32)


def place_of_block():
    return [(p, b) for p, blocks in enumerate(PIECES) for b in range(blocks)]


def on_diagonal(unit):
    shape = (UNIT, BLOCK)
    return lax.broadcasted_iota(jnp.int32, shape, 0) + unit * UNIT == lax.broadcasted_iota(
        jnp.int32, shape, 1
    )


def kept(order, stage):
    gone = sum(order[: stage + 1])
    return [by for by in range(PLACES) if not by & gone]


def sent(order, stage):
    return [by | order[stage] for by in kept(order, stage)]


def rows_sent(group, stage):
    blocks, order = group
    return len(blocks[0]) * len(sent(order, stage)) * UNIT


def exchange_shapes(group, stage):
    blocks, order = group
    return [
        jax.ShapeDtypeStruct((len(blocks[0]), len(kept(order, stage)), UNIT, BLOCK), F32),
        jax.ShapeDtypeStruct((rows_sent(group, stage) + TAIL, BLOCK), BF16),
    ]


def write_sent(send, tail, e, parts, units, flag):
    left = jnp.zeros((1, BLOCK), F32)
    for n, (part, unit) in enumerate(zip(parts, units)):
        near = part.astype(BF16)
        row = (e * len(parts) + n) * UNIT
        send[pl.ds(row if isinstance(row, int) else pl.multiple_of(row, UNIT), UNIT), :] = near
        if flag is not None:
            rest = jnp.where(on_diagonal(unit), part - near.astype(F32), 0.0)
            left += jnp.sum(rest, axis=0, keepdims=True)
    if flag is not None:
        tail[pl.ds(e, 1), :] = left * flag


def gram_kernel(groups, pieces, *refs):
    where = place_of_block()[: sum(PIECES[:pieces])]
    inputs, refs = refs[: 2 * pieces], refs[2 * pieces :]
    count = 2 * len(groups)
    outs, refs = refs[:count], refs[count:]
    keeps, sends, refs = refs[0:count:2], refs[1:count:2], refs[count:]
    tails, (panel, arrived, gone) = refs[: len(groups)], refs[len(groups) :]
    y, x, core, high, low = place()
    for source in range(2):
        for i, (p, b) in enumerate(where):
            for step in range(4):
                spot = pl.multiple_of(slab_of(high, low, step) * BAND, BAND)
                pltpu.make_async_copy(
                    inputs[source * pieces + p].at[step, pl.ds(b * BAND, BAND), :],
                    panel.at[i, pl.ds(spot, BAND), pl.ds(source * GROUP, GROUP)],
                    arrived,
                ).start()
    for tail in tails:
        tail[...] = jnp.zeros_like(tail)
    pltpu.make_async_copy(panel, panel, arrived).wait()
    for g, group in enumerate(groups):
        blocks, order = group
        keep, send, tail = keeps[g], sends[g], tails[g]
        size = len(sent(order, 0)) * UNIT
        diagonal = blocks[0][0][1] == 0

        def block(e, carry):
            at = [
                jnp.where(core == 0, lookup(e, [b[n] for b in blocks[0]]), lookup(e, [b[n] for b in blocks[1]]))
                for n in range(2)
            ]
            i, j = at[0], lax.rem(at[0] + at[1], BLOCKS)
            rows = [
                panel[i, pl.ds(pl.multiple_of(place_of(x, y, low, by) * UNIT, UNIT), UNIT), :]
                for by in range(PLACES)
            ]
            got = dot(jnp.concatenate(rows), panel[j], ((1,), (1,)))
            for n, by in enumerate(kept(order, 0)):
                keep[e, n] = got[by * UNIT : (by + 1) * UNIT]
            parts = [got[by * UNIT : (by + 1) * UNIT] for by in sent(order, 0)]
            units = [place_of(x, y, low, by) for by in sent(order, 0)]
            write_sent(send, tail, e, parts, units, (core == 0).astype(F32) if diagonal else None)
            pltpu.make_async_copy(keep.at[e], outs[2 * g].at[e], gone.at[2 * g]).start()
            rows = pl.ds(pl.multiple_of(e * size, size), size)
            pltpu.make_async_copy(
                send.at[rows, :], outs[2 * g + 1].at[rows, :], gone.at[2 * g + 1]
            ).start()
            return carry

        lax.fori_loop(0, len(blocks[0]), block, 0)
        rows = pl.ds(rows_sent(group, 0), TAIL)
        send[rows, :] = tail[...].astype(BF16)
        pltpu.make_async_copy(
            send.at[rows, :], outs[2 * g + 1].at[rows, :], gone.at[2 * g + 1]
        ).start()
    for g in range(len(groups)):
        for n, ref in ((2 * g, keeps[g]), (2 * g + 1, sends[g])):
            pltpu.make_async_copy(ref, outs[n], gone.at[n]).wait()


def add_kernel(groups, stage, before, *refs):
    last = stage == 2
    count = 2 * len(groups)
    keeps, gots, refs = refs[0:count:2], refs[1:count:2], refs[count:]
    early, outs = refs[:before], refs[before:]
    y, x, core, high, low = place()
    for g, group in enumerate(groups):
        blocks, order = group
        keep, got = keeps[g], gots[g]
        held = kept(order, stage)
        diagonal = blocks[0][0][1] == 0
        left = got[pl.ds(rows_sent(group, stage), TAIL), :].astype(F32)
        skip = 0
        if last and before:
            skip = 1
            outs[g][0] = early[0][g]
        if not last:
            nxt, send, tail = outs[2 * g], outs[2 * g + 1], outs[count + g]
            tail[...] = jnp.zeros_like(tail)
        for e in range(len(blocks[0])):
            sums = {}
            for n, by in enumerate(held):
                row = (e * len(held) + n) * UNIT
                here = keep[e, n] + got[row : row + UNIT, :].astype(F32)
                if diagonal:
                    unit = place_of(x, y, low, by)
                    here += jnp.where(on_diagonal(unit), left[e : e + 1, :], 0.0)
                sums[by] = here
            if last:
                outs[g][skip + e] = sums[0].astype(BF16)
                continue
            for n, by in enumerate(kept(order, stage + 1)):
                nxt[e, n] = sums[by]
            going = sent(order, stage + 1)
            units = [place_of(x, y, low, by) for by in going]
            flag = (core == 0).astype(F32) if diagonal else None
            write_sent(send, tail, e, [sums[by] for by in going], units, flag)
        if not last:
            send[pl.ds(rows_sent(group, stage + 1), TAIL), :] = tail[...].astype(BF16)


def gram_call(groups, own, beside):
    inputs = own + beside
    rows = sum(PIECES[: len(own)])
    shapes = [shape for group in groups for shape in exchange_shapes(group, 0)]
    return pl.pallas_call(
        functools.partial(gram_kernel, groups, len(own)),
        out_shape=shapes,
        in_specs=[pl.BlockSpec(memory_space=pl.ANY)] * len(inputs),
        out_specs=[pl.BlockSpec(memory_space=pl.ANY)] * len(shapes),
        scratch_shapes=[pltpu.VMEM(shape.shape, shape.dtype) for shape in shapes]
        + [pltpu.VMEM((TAIL, BLOCK), F32)] * len(groups)
        + [
            pltpu.VMEM((rows, BLOCK, 2 * GROUP), BF16),
            pltpu.SemaphoreType.DMA,
            pltpu.SemaphoreType.DMA((len(shapes),)),
        ],
        compiler_params=pltpu.CompilerParams(vmem_limit_bytes=GRAM_VMEM),
        cost_estimate=pl.CostEstimate(
            flops=sum(len(group[0][0]) for group in groups) * BLOCK * BLOCK,
            bytes_accessed=rows << 16,
            transcendentals=0,
        ),
        name="gram",
    )(*inputs)


def add_call(groups, stage, inputs, early):
    if stage < 2:
        shapes = [shape for group in groups for shape in exchange_shapes(group, stage + 1)]
        scratch = [pltpu.VMEM((TAIL, BLOCK), F32)] * len(groups)
        early = []
    else:
        extra = 1 if early else 0
        shapes = [
            jax.ShapeDtypeStruct((len(blocks[0]) + extra, UNIT, BLOCK), BF16) for blocks, _ in groups
        ]
        scratch = []
    inputs = inputs + early
    return pl.pallas_call(
        functools.partial(add_kernel, groups, stage, len(early)),
        out_shape=shapes,
        in_specs=[pl.BlockSpec(memory_space=pltpu.VMEM)] * len(inputs),
        out_specs=[pl.BlockSpec(memory_space=pltpu.VMEM)] * len(shapes),
        scratch_shapes=scratch,
        compiler_params=pltpu.CompilerParams(vmem_limit_bytes=40 << 20),
        cost_estimate=pl.CostEstimate(flops=1 << 16, bytes_accessed=1 << 16, transcendentals=0),
        name="add",
    )(*inputs)


def summed(groups, parts, stage, early=()):
    inputs = []
    for g, (_, order) in enumerate(groups):
        inputs += [parts[2 * g], MOVES[order[stage]](parts[2 * g + 1])]
    return add_call(groups, stage, inputs, list(early))


def gathered(mine):
    thirds = range(3)

    def move(stage, pieces):
        return [
            ([by ^ ORDERS[t][stage] for by in pieces[t][0]], MOVES[ORDERS[t][stage]](pieces[t][1]))
            for t in thirds
        ]

    def wave(*groups):
        return lax.optimization_barrier(groups)

    out = []

    def place_in(pieces, core):
        out.extend(((t, bys, core), piece) for t, (bys, piece) in enumerate(pieces))

    def across(pieces):
        place_in(pieces, 0)
        place_in([(bys, over_core(piece)) for bys, piece in pieces], 1)

    def merge(a, b):
        return [(p[0] + q[0], jnp.concatenate([p[1], q[1]])) for p, q in zip(a, b)]

    def unkeyed(pieces):
        return [piece for _, piece in pieces]

    def keyed(pieces, arrays):
        return [(bys, array) for (bys, _), array in zip(pieces, arrays)]

    def ordered(*groups):
        done = wave([unkeyed(group) for group in groups], [piece for _, piece in out])
        out[:] = [(key, piece) for (key, _), piece in zip(out, done[1])]
        return [keyed(group, arrays) for group, arrays in zip(groups, done[0])]

    own = [([0], piece) for piece in mine]
    (pair,) = ordered(merge(own, move(0, own)))
    second = move(1, pair)
    across(pair)
    pair, second = ordered(pair, second)
    third_a = move(2, pair)
    across(second)
    second, third_a = ordered(second, third_a)
    third_b = move(2, second)
    across(third_a)
    (third_b,) = ordered(third_b)
    across(third_b)
    return out


def step_kernel(keys, part, *refs):
    gram_pieces = refs[: len(keys)]
    refs = refs[len(keys) :]
    iter_pieces = refs[: len(PIECES)]
    outs = refs[len(PIECES) : len(PIECES) + 4]
    gram, panel, first, total, result, here, there, gone = refs[len(PIECES) + 4 :]
    y, x, core, high, low = place()
    for i, (p, b) in enumerate(place_of_block()):
        for step in range(4):
            pltpu.make_async_copy(
                iter_pieces[p].at[step, pl.ds(b * BAND, BAND), pl.ds(part * WIDE, WIDE)],
                panel.at[i, slab_of(high, low, step)],
                there,
            ).start()
    for (third, bys, other), piece in zip(keys, gram_pieces):
        lo, hi = THIRDS[third]
        for n, by in enumerate(bys):
            pltpu.make_async_copy(
                piece.at[n],
                gram.at[
                    pl.ds(flip(core, other) * MINE + lo, hi - lo), place_of(x, y, low, by)
                ],
                here,
            ).start()
    pltpu.make_async_copy(panel, panel, there).wait()
    pltpu.make_async_copy(gram, gram, here).wait()

    def rows_of(i):
        return pl.ds(pl.multiple_of(i * BLOCK, BLOCK), BLOCK)

    def block(d, i):
        return gram[lookup(i, [SPOT[n, d] for n in range(BLOCKS)])].reshape(BLOCK, BLOCK)

    def apply(source, i):
        got = dot(block(0, i), source(i), ((1,), (0,)))
        for d in range(1, DIAGS):
            j = lax.rem(i + d, BLOCKS)
            got += dot(block(d, i), source(j), ((1,), (0,)))
            j = lax.rem(i + BLOCKS - d, BLOCKS)
            got += dot(block(d, j), source(j), ((0,), (0,)))
        return got

    def iter_rows(i):
        return panel[i].reshape(BLOCK, WIDE)

    def one(i, carry):
        got = apply(iter_rows, i)
        first[rows_of(i), :] = got.astype(BF16)
        total[rows_of(i), :] = quint_a * iter_rows(i).astype(F32) + quint_b * got
        return carry

    def two(i, carry):
        got = apply(lambda j: first[rows_of(j), :], i)
        result[i] = (total[rows_of(i), :] + quint_c * got).astype(BF16).reshape(4, BAND, WIDE)
        return carry

    lax.fori_loop(0, BLOCKS, one, 0)
    lax.fori_loop(0, BLOCKS, two, 0)
    copies = []
    for step in range(4):
        copies.append(
            pltpu.make_async_copy(
                result.at[:, slab_of(y, low, step)], outs[step], gone.at[step]
            )
        )
        copies[-1].start()
    for copy in copies:
        copy.wait()


def step_call(keys, gram_pieces, iter_pieces, part):
    count = len(gram_pieces) + len(iter_pieces)
    return pl.pallas_call(
        functools.partial(step_kernel, keys, part),
        out_shape=[jax.ShapeDtypeStruct((BLOCKS, BAND, WIDE), BF16)] * 4,
        in_specs=[pl.BlockSpec(memory_space=pl.ANY)] * count,
        out_specs=[pl.BlockSpec(memory_space=pl.ANY)] * 4,
        scratch_shapes=[
            pltpu.VMEM((2 * MINE, PLACES, UNIT, BLOCK), BF16),
            pltpu.VMEM((BLOCKS, 4, BAND, WIDE), BF16),
            pltpu.VMEM((ORDER, WIDE), BF16),
            pltpu.VMEM((ORDER, WIDE), F32),
            pltpu.VMEM((BLOCKS, 4, BAND, WIDE), BF16),
            pltpu.SemaphoreType.DMA,
            pltpu.SemaphoreType.DMA,
            pltpu.SemaphoreType.DMA((4,)),
        ],
        compiler_params=pltpu.CompilerParams(vmem_limit_bytes=STEP_VMEM),
        cost_estimate=pl.CostEstimate(
            flops=4 * ORDER * ORDER * WIDE, bytes_accessed=20 << 20, transcendentals=0
        ),
        name="step",
    )(*gram_pieces, *iter_pieces)


def pick(a, at, size, axis):
    return lax.dynamic_slice_in_dim(a, at, size, axis)


def panels(iterate):
    y, x, core, high, low = place()
    aligned = y == high
    starts = [sum(HOPS[:n]) * BAND for n in range(len(HOPS))]

    def cast(n, at):
        size = (HOPS[n] * BAND, 2 * GROUP)
        return lax.dynamic_slice(iterate, (starts[n], at * 2 * GROUP), size).astype(BF16)

    def chunks(keep, other):
        near, far = jnp.where(aligned, keep, other), jnp.where(aligned, other, keep)
        return [
            pick(far if step >> 1 else near, flip(low, step & 1) * GROUP, GROUP, 1)
            for step in range(4)
        ]

    def travel(ready):
        return [ready[0]] + [over_z(ready[step], step) for step in (1, 2, 3)]

    def joined(pieces):
        return jnp.stack([jnp.concatenate(slab) for slab in zip(*pieces)])

    done = []
    keep, other = cast(0, y), over_y(cast(0, 1 - y))
    for n in range(len(HOPS) - 1):
        ahead = [cast(n + 1, y), cast(n + 1, 1 - y)]
        ready, ahead, done = lax.optimization_barrier((chunks(keep, other), ahead, done))
        done.append(travel(ready))
        keep, other = ahead[0], over_y(ahead[1])
    ready = chunks(keep, other)
    own = [joined(done)]
    done, parts, start = [], None, 0
    for n, blocks in enumerate(LAST):
        stop = start + blocks * BAND
        now, ready, done, own, parts = lax.optimization_barrier(
            ([chunk[start:stop] for chunk in ready], ready, done, own, parts)
        )
        start = stop
        done.append(travel(now))
        if n == 0:
            beside = [over_core(own[0])]
            parts = gram_call(EARLY_GROUPS, own, beside)
        else:
            parts = summed(EARLY_GROUPS, parts, n - 1)
    out = (FACTOR * quint_a) * (iterate - lax.reduce_precision(iterate, 8, 7))
    out, parts, done = lax.optimization_barrier((out, parts, done))
    own.append(joined(done))
    beside.append(over_core(own[1]))
    return own, beside, summed(EARLY_GROUPS, parts, 2), out


def shards_cube(iterate):
    y, x, core, high, low = place()
    own, beside, early, out = panels(iterate)
    mine = gram_call(LATE_GROUPS, own, beside)
    for stage in range(3):
        mine = summed(LATE_GROUPS, mine, stage, early)
    entries = gathered([piece[None] for piece in mine])
    keys = [key for key, _ in entries]
    gram_pieces = [piece.reshape(-1, *piece.shape[-3:]) for _, piece in entries]

    before = None
    for part in range(HALVES):
        slabs = step_call(keys, gram_pieces, own, part)
        if before is not None:
            slabs, before = lax.optimization_barrier((slabs, before))
        got = [home(slabs[step], step) for step in range(4)]
        for step in range(4):
            at = slab_of(high, low, step) * GROUP + part * WIDE
            piece = FACTOR * got[step].reshape(SLAB, WIDE).astype(F32)
            out = lax.dynamic_update_slice_in_dim(out, pick(out, at, WIDE, 1) + piece, at, 1)
        before = got
    return out


def solution(mesh):
    shards = shards_cube if dict(mesh.shape) == {"mats": 2, "col": 4, "row": 4} else shards_rows
    in_specs = (P(("mats", "row"), "col"),)
    out_specs = P(("mats", "row"), "col")
    return jax.shard_map(shards, mesh=mesh, in_specs=in_specs, out_specs=out_specs, check_vma=False)
```

```python
import functools
import math

import jax
import jax.numpy as jnp
from jax import lax
from jax.experimental import pallas as pl
from jax.experimental.pallas import tpu as pltpu
from jax.sharding import PartitionSpec as P

ORDER = 3584
COLS = 8192

BF16 = jnp.bfloat16
F32 = jnp.float32

quint_a = 3.4445
quint_b = -4.775
quint_c = 2.0315

FACTOR = 0.2 * math.sqrt(max(ORDER, COLS))

BLOCK = 512
BLOCKS = ORDER // BLOCK
DIAGS = 4
MINE = DIAGS * BLOCKS // 2
THIRDS = ((0, 5), (5, 10), (10, 14))
PLACES = 8
UNIT = BLOCK // PLACES
TAIL = 16
SLAB = ORDER // 4
BAND = SLAB // BLOCKS
GROUP = COLS // 16
HOPS = (1, 2, 4)
LAST = (2, 2)
PIECES = (3, 4)
HALVES = 2
WIDE = GROUP // HALVES
GRAM_VMEM = 28 << 20
STEP_VMEM = 60 << 20


def shards_rows(iterate):
    iter_bf = iterate.astype(BF16)
    column_panel = lax.all_gather(iter_bf, "row", axis=0, tiled=True)
    gram_part = lax.psum_scatter(
        lax.dot_general(
            column_panel, iter_bf, (((1,), (1,)), ((), ())), preferred_element_type=F32
        ),
        "col",
        scatter_dimension=0,
        tiled=True,
    )
    gram_cols = lax.all_gather(gram_part.astype(BF16), "col", axis=0, tiled=True)
    first = lax.dot_general(
        gram_cols, column_panel, (((0,), (0,)), ((), ())), preferred_element_type=F32
    )
    second = lax.dot_general(
        gram_cols,
        lax.all_gather(first.astype(BF16), "row", axis=0, tiled=True),
        (((0,), (0,)), ((), ())),
        preferred_element_type=F32,
    )
    return FACTOR * (quint_a * iterate + quint_b * first + quint_c * second)


def flip(bit, by):
    return 1 - bit if by else bit


def place():
    col = lax.axis_index("col")
    row = lax.axis_index("row")
    return lax.axis_index("mats"), col // 2, col % 2, row // 2, row % 2


def slab_of(high, low, step):
    return 2 * flip(high, step >> 1) + flip(low, step & 1)


def place_of(x, y, low, by):
    return 4 * flip(x, by >> 2) + 2 * flip(y, by >> 1 & 1) + flip(low, by & 1)


def over_x(a):
    return lax.ppermute(a, "col", [(0, 2), (1, 3), (2, 0), (3, 1)])


def over_core(a):
    return lax.ppermute(a, "col", [(0, 1), (1, 0), (2, 3), (3, 2)])


def over_y(a):
    return lax.ppermute(a, "mats", [(0, 1), (1, 0)])


def over_z(a, step=1):
    return lax.ppermute(a, "row", [(z, z ^ step) for z in range(4)])


MOVES = {4: over_x, 2: over_y, 1: over_z}
ORDERS = ((4, 2, 1), (2, 1, 4), (1, 4, 2))

EARLY = (((0, 0), (1, 0), (2, 0)), ((0, 1), (1, 1), (0, 2)))
LATE = [
    (i, d) for d in range(DIAGS) for i in range(BLOCKS) if (i, d) not in EARLY[0] + EARLY[1]
]
LATE = (LATE[: MINE - 3], LATE[MINE - 3 :])
EARLY_GROUPS = tuple(
    ([core[lo:hi] for core in EARLY], order)
    for (lo, hi), order in (((0, 3), (4, 2, 1)),)
)
LATE_GROUPS = tuple(
    ([core[lo:hi] for core in LATE], order)
    for (lo, hi), order in zip(((0, 4), (4, 8), (8, 11)), ORDERS)
)
SPOT = {
    block: core * MINE + THIRDS[third][0] + n
    for core in range(2)
    for third in range(3)
    for n, block in enumerate([EARLY[core][third]] + LATE_GROUPS[third][0][core])
}


def lookup(index, values):
    got = values[0]
    for n, value in enumerate(values[1:], 1):
        got = jnp.where(index == n, value, got)
    return got


def home(a, step):
    pairs = []
    for y in range(2):
        for z in range(4):
            part, slab = z // 2, (2 * y + z % 2) ^ step
            pairs.append((4 * y + z, 4 * part + slab))
    return lax.ppermute(a, ("mats", "row"), pairs)


def dot(a, b, dims):
    return lax.dot_general(a, b, (dims, ((), ())), preferred_element_type=F32)


def place_of_block():
    return [(p, b) for p, blocks in enumerate(PIECES) for b in range(blocks)]


def on_diagonal(unit):
    shape = (UNIT, BLOCK)
    return lax.broadcasted_iota(jnp.int32, shape, 0) + unit * UNIT == lax.broadcasted_iota(
        jnp.int32, shape, 1
    )


def kept(order, stage):
    gone = sum(order[: stage + 1])
    return [by for by in range(PLACES) if not by & gone]


def sent(order, stage):
    return [by | order[stage] for by in kept(order, stage)]


def rows_sent(group, stage):
    blocks, order = group
    return len(blocks[0]) * len(sent(order, stage)) * UNIT


def exchange_shapes(group, stage):
    blocks, order = group
    return [
        jax.ShapeDtypeStruct((len(blocks[0]), len(kept(order, stage)), UNIT, BLOCK), F32),
        jax.ShapeDtypeStruct((rows_sent(group, stage) + TAIL, BLOCK), BF16),
    ]


def write_sent(send, tail, e, parts, units, flag):
    left = jnp.zeros((1, BLOCK), F32)
    for n, (part, unit) in enumerate(zip(parts, units)):
        near = part.astype(BF16)
        row = (e * len(parts) + n) * UNIT
        send[pl.ds(row if isinstance(row, int) else pl.multiple_of(row, UNIT), UNIT), :] = near
        if flag is not None:
            rest = jnp.where(on_diagonal(unit), part - near.astype(F32), 0.0)
            left += jnp.sum(rest, axis=0, keepdims=True)
    if flag is not None:
        tail[pl.ds(e, 1), :] = left * flag


def gram_kernel(groups, pieces, *refs):
    where = place_of_block()[: sum(PIECES[:pieces])]
    inputs, refs = refs[: 2 * pieces], refs[2 * pieces :]
    count = 2 * len(groups)
    outs, refs = refs[:count], refs[count:]
    keeps, sends, refs = refs[0:count:2], refs[1:count:2], refs[count:]
    tails, (panel, arrived, gone) = refs[: len(groups)], refs[len(groups) :]
    y, x, core, high, low = place()
    for source in range(2):
        for i, (p, b) in enumerate(where):
            for step in range(4):
                spot = pl.multiple_of(slab_of(high, low, step) * BAND, BAND)
                pltpu.make_async_copy(
                    inputs[source * pieces + p].at[step, pl.ds(b * BAND, BAND), :],
                    panel.at[i, pl.ds(spot, BAND), pl.ds(source * GROUP, GROUP)],
                    arrived,
                ).start()
    for tail in tails:
        tail[...] = jnp.zeros_like(tail)
    pltpu.make_async_copy(panel, panel, arrived).wait()
    for g, group in enumerate(groups):
        blocks, order = group
        keep, send, tail = keeps[g], sends[g], tails[g]
        size = len(sent(order, 0)) * UNIT
        diagonal = blocks[0][0][1] == 0

        def block(e, carry):
            at = [
                jnp.where(core == 0, lookup(e, [b[n] for b in blocks[0]]), lookup(e, [b[n] for b in blocks[1]]))
                for n in range(2)
            ]
            i, j = at[0], lax.rem(at[0] + at[1], BLOCKS)
            rows = [
                panel[i, pl.ds(pl.multiple_of(place_of(x, y, low, by) * UNIT, UNIT), UNIT), :]
                for by in range(PLACES)
            ]
            got = dot(jnp.concatenate(rows), panel[j], ((1,), (1,)))
            for n, by in enumerate(kept(order, 0)):
                keep[e, n] = got[by * UNIT : (by + 1) * UNIT]
            parts = [got[by * UNIT : (by + 1) * UNIT] for by in sent(order, 0)]
            units = [place_of(x, y, low, by) for by in sent(order, 0)]
            write_sent(send, tail, e, parts, units, (core == 0).astype(F32) if diagonal else None)
            pltpu.make_async_copy(keep.at[e], outs[2 * g].at[e], gone.at[2 * g]).start()
            rows = pl.ds(pl.multiple_of(e * size, size), size)
            pltpu.make_async_copy(
                send.at[rows, :], outs[2 * g + 1].at[rows, :], gone.at[2 * g + 1]
            ).start()
            return carry

        lax.fori_loop(0, len(blocks[0]), block, 0)
        rows = pl.ds(rows_sent(group, 0), TAIL)
        send[rows, :] = tail[...].astype(BF16)
        pltpu.make_async_copy(
            send.at[rows, :], outs[2 * g + 1].at[rows, :], gone.at[2 * g + 1]
        ).start()
    for g in range(len(groups)):
        for n, ref in ((2 * g, keeps[g]), (2 * g + 1, sends[g])):
            pltpu.make_async_copy(ref, outs[n], gone.at[n]).wait()


def add_kernel(groups, stage, before, *refs):
    last = stage == 2
    count = 2 * len(groups)
    keeps, gots, refs = refs[0:count:2], refs[1:count:2], refs[count:]
    early, outs = refs[:before], refs[before:]
    y, x, core, high, low = place()
    for g, group in enumerate(groups):
        blocks, order = group
        keep, got = keeps[g], gots[g]
        held = kept(order, stage)
        diagonal = blocks[0][0][1] == 0
        left = got[pl.ds(rows_sent(group, stage), TAIL), :].astype(F32)
        skip = 0
        if last and before:
            skip = 1
            outs[g][0] = early[0][g]
        if not last:
            nxt, send, tail = outs[2 * g], outs[2 * g + 1], outs[count + g]
            tail[...] = jnp.zeros_like(tail)
        for e in range(len(blocks[0])):
            sums = {}
            for n, by in enumerate(held):
                row = (e * len(held) + n) * UNIT
                here = keep[e, n] + got[row : row + UNIT, :].astype(F32)
                if diagonal:
                    unit = place_of(x, y, low, by)
                    here += jnp.where(on_diagonal(unit), left[e : e + 1, :], 0.0)
                sums[by] = here
            if last:
                outs[g][skip + e] = sums[0].astype(BF16)
                continue
            for n, by in enumerate(kept(order, stage + 1)):
                nxt[e, n] = sums[by]
            going = sent(order, stage + 1)
            units = [place_of(x, y, low, by) for by in going]
            flag = (core == 0).astype(F32) if diagonal else None
            write_sent(send, tail, e, [sums[by] for by in going], units, flag)
        if not last:
            send[pl.ds(rows_sent(group, stage + 1), TAIL), :] = tail[...].astype(BF16)


def gram_call(groups, own, beside):
    inputs = own + beside
    rows = sum(PIECES[: len(own)])
    shapes = [shape for group in groups for shape in exchange_shapes(group, 0)]
    return pl.pallas_call(
        functools.partial(gram_kernel, groups, len(own)),
        out_shape=shapes,
        in_specs=[pl.BlockSpec(memory_space=pl.ANY)] * len(inputs),
        out_specs=[pl.BlockSpec(memory_space=pl.ANY)] * len(shapes),
        scratch_shapes=[pltpu.VMEM(shape.shape, shape.dtype) for shape in shapes]
        + [pltpu.VMEM((TAIL, BLOCK), F32)] * len(groups)
        + [
            pltpu.VMEM((rows, BLOCK, 2 * GROUP), BF16),
            pltpu.SemaphoreType.DMA,
            pltpu.SemaphoreType.DMA((len(shapes),)),
        ],
        compiler_params=pltpu.CompilerParams(vmem_limit_bytes=GRAM_VMEM),
        cost_estimate=pl.CostEstimate(
            flops=len(own) // 2 * MINE * 2 * BLOCK * BLOCK * 2 * GROUP,
            bytes_accessed=rows << 16,
            transcendentals=0,
        ),
        name="gram",
    )(*inputs)


def add_call(groups, stage, inputs, early):
    if stage < 2:
        shapes = [shape for group in groups for shape in exchange_shapes(group, stage + 1)]
        scratch = [pltpu.VMEM((TAIL, BLOCK), F32)] * len(groups)
        early = []
    else:
        extra = 1 if early else 0
        shapes = [
            jax.ShapeDtypeStruct((len(blocks[0]) + extra, UNIT, BLOCK), BF16) for blocks, _ in groups
        ]
        scratch = []
    inputs = inputs + early
    return pl.pallas_call(
        functools.partial(add_kernel, groups, stage, len(early)),
        out_shape=shapes,
        in_specs=[pl.BlockSpec(memory_space=pltpu.VMEM)] * len(inputs),
        out_specs=[pl.BlockSpec(memory_space=pltpu.VMEM)] * len(shapes),
        scratch_shapes=scratch,
        compiler_params=pltpu.CompilerParams(vmem_limit_bytes=40 << 20),
        cost_estimate=pl.CostEstimate(flops=1 << 16, bytes_accessed=1 << 16, transcendentals=0),
        name="add",
    )(*inputs)


def summed(groups, parts, stage, early=(), beside=None):
    inputs = []
    for g, (_, order) in enumerate(groups):
        inputs += [parts[2 * g], MOVES[order[stage]](parts[2 * g + 1])]
    if beside is not None:
        inputs, beside = lax.optimization_barrier((inputs, beside))
        return add_call(groups, stage, inputs, list(early)), beside
    return add_call(groups, stage, inputs, list(early))


def gathered(mine):
    thirds = range(3)

    def move(stage, pieces):
        return [
            ([by ^ ORDERS[t][stage] for by in pieces[t][0]], MOVES[ORDERS[t][stage]](pieces[t][1]))
            for t in thirds
        ]

    def wave(*groups):
        return lax.optimization_barrier(groups)

    out = []

    def place_in(pieces, core):
        out.extend(((t, bys, core), piece) for t, (bys, piece) in enumerate(pieces))

    def across(pieces):
        place_in(pieces, 0)
        place_in([(bys, over_core(piece)) for bys, piece in pieces], 1)

    def merge(a, b):
        return [(p[0] + q[0], jnp.concatenate([p[1], q[1]])) for p, q in zip(a, b)]

    def unkeyed(pieces):
        return [piece for _, piece in pieces]

    def keyed(pieces, arrays):
        return [(bys, array) for (bys, _), array in zip(pieces, arrays)]

    def ordered(*groups):
        done = wave([unkeyed(group) for group in groups], [piece for _, piece in out])
        out[:] = [(key, piece) for (key, _), piece in zip(out, done[1])]
        return [keyed(group, arrays) for group, arrays in zip(groups, done[0])]

    own = [([0], piece) for piece in mine]
    (pair,) = ordered(merge(own, move(0, own)))
    second = move(1, pair)
    across(pair)
    pair, second = ordered(pair, second)
    third_a = move(2, pair)
    across(second)
    second, third_a = ordered(second, third_a)
    third_b = move(2, second)
    across(third_a)
    (third_b,) = ordered(third_b)
    across(third_b)
    return out


def step_kernel(keys, part, *refs):
    gram_pieces = refs[: len(keys)]
    refs = refs[len(keys) :]
    iter_pieces = refs[: len(PIECES)]
    outs = refs[len(PIECES) : len(PIECES) + 4]
    gram, panel, first, total, result, here, there, gone = refs[len(PIECES) + 4 :]
    y, x, core, high, low = place()
    for i, (p, b) in enumerate(place_of_block()):
        for step in range(4):
            pltpu.make_async_copy(
                iter_pieces[p].at[step, pl.ds(b * BAND, BAND), pl.ds(part * WIDE, WIDE)],
                panel.at[i, slab_of(high, low, step)],
                there,
            ).start()
    for (third, bys, other), piece in zip(keys, gram_pieces):
        lo, hi = THIRDS[third]
        for n, by in enumerate(bys):
            pltpu.make_async_copy(
                piece.at[n],
                gram.at[
                    pl.ds(flip(core, other) * MINE + lo, hi - lo), place_of(x, y, low, by)
                ],
                here,
            ).start()
    pltpu.make_async_copy(panel, panel, there).wait()
    pltpu.make_async_copy(gram, gram, here).wait()

    def rows_of(i):
        return pl.ds(pl.multiple_of(i * BLOCK, BLOCK), BLOCK)

    def block(d, i):
        return gram[lookup(i, [SPOT[n, d] for n in range(BLOCKS)])].reshape(BLOCK, BLOCK)

    def apply(source, i):
        got = dot(block(0, i), source(i), ((1,), (0,)))
        for d in range(1, DIAGS):
            j = lax.rem(i + d, BLOCKS)
            got += dot(block(d, i), source(j), ((1,), (0,)))
            j = lax.rem(i + BLOCKS - d, BLOCKS)
            got += dot(block(d, j), source(j), ((0,), (0,)))
        return got

    def iter_rows(i):
        return panel[i].reshape(BLOCK, WIDE)

    def one(i, carry):
        got = apply(iter_rows, i)
        first[rows_of(i), :] = got.astype(BF16)
        total[rows_of(i), :] = quint_a * iter_rows(i).astype(F32) + quint_b * got
        return carry

    def two(i, carry):
        got = apply(lambda j: first[rows_of(j), :], i)
        result[i] = (total[rows_of(i), :] + quint_c * got).astype(BF16).reshape(4, BAND, WIDE)
        return carry

    lax.fori_loop(0, BLOCKS, one, 0)
    lax.fori_loop(0, BLOCKS, two, 0)
    copies = []
    for step in range(4):
        copies.append(
            pltpu.make_async_copy(
                result.at[:, slab_of(y, low, step)], outs[step], gone.at[step]
            )
        )
        copies[-1].start()
    for copy in copies:
        copy.wait()


def step_call(keys, gram_pieces, iter_pieces, part):
    count = len(gram_pieces) + len(iter_pieces)
    return pl.pallas_call(
        functools.partial(step_kernel, keys, part),
        out_shape=[jax.ShapeDtypeStruct((BLOCKS, BAND, WIDE), BF16)] * 4,
        in_specs=[pl.BlockSpec(memory_space=pl.ANY)] * count,
        out_specs=[pl.BlockSpec(memory_space=pl.ANY)] * 4,
        scratch_shapes=[
            pltpu.VMEM((2 * MINE, PLACES, UNIT, BLOCK), BF16),
            pltpu.VMEM((BLOCKS, 4, BAND, WIDE), BF16),
            pltpu.VMEM((ORDER, WIDE), BF16),
            pltpu.VMEM((ORDER, WIDE), F32),
            pltpu.VMEM((BLOCKS, 4, BAND, WIDE), BF16),
            pltpu.SemaphoreType.DMA,
            pltpu.SemaphoreType.DMA,
            pltpu.SemaphoreType.DMA((4,)),
        ],
        compiler_params=pltpu.CompilerParams(vmem_limit_bytes=STEP_VMEM),
        cost_estimate=pl.CostEstimate(
            flops=4 * ORDER * ORDER * WIDE, bytes_accessed=20 << 20, transcendentals=0
        ),
        name="step",
    )(*gram_pieces, *iter_pieces)


def pick(a, at, size, axis):
    return lax.dynamic_slice_in_dim(a, at, size, axis)


def panels(iterate):
    y, x, core, high, low = place()
    aligned = y == high
    starts = [sum(HOPS[:n]) * BAND for n in range(len(HOPS))]

    def cast(n, at):
        size = (HOPS[n] * BAND, 2 * GROUP)
        return lax.dynamic_slice(iterate, (starts[n], at * 2 * GROUP), size).astype(BF16)

    def chunks(keep, other):
        near, far = jnp.where(aligned, keep, other), jnp.where(aligned, other, keep)
        return [
            pick(far if step >> 1 else near, flip(low, step & 1) * GROUP, GROUP, 1)
            for step in range(4)
        ]

    def travel(ready):
        return [ready[0]] + [over_z(ready[step], step) for step in (1, 2, 3)]

    def joined(pieces):
        return jnp.stack([jnp.concatenate(slab) for slab in zip(*pieces)])

    done = []
    keep, other = cast(0, y), over_y(cast(0, 1 - y))
    ahead = [(cast(n, y), cast(n, 1 - y)) for n in range(1, len(HOPS))]
    for n in range(len(HOPS) - 1):
        ready, ahead, done = lax.optimization_barrier((chunks(keep, other), ahead, done))
        done.append(travel(ready))
        keep, other = ahead[n][0], over_y(ahead[n][1])
    ready = chunks(keep, other)
    own = [joined(done)]
    done, parts, start = [], None, 0
    for n, blocks in enumerate(LAST):
        stop = start + blocks * BAND
        now, ready, done, own, parts = lax.optimization_barrier(
            ([chunk[start:stop] for chunk in ready], ready, done, own, parts)
        )
        start = stop
        done.append(travel(now))
        if n == 0:
            beside = [over_core(own[0])]
            parts = gram_call(EARLY_GROUPS, own, beside)
        else:
            parts = summed(EARLY_GROUPS, parts, n - 1)
    out = (FACTOR * quint_a) * (iterate - lax.reduce_precision(iterate, 8, 7))
    out, parts, done = lax.optimization_barrier((out, parts, done))
    own.append(joined(done))
    beside.append(over_core(own[1]))
    return own, beside, parts, out


def shards_cube(iterate):
    y, x, core, high, low = place()
    own, beside, early, out = panels(iterate)
    early, mine = summed(EARLY_GROUPS, early, 1, beside=gram_call(LATE_GROUPS, own, beside))
    early = summed(EARLY_GROUPS, early, 2)
    mine, early = lax.optimization_barrier((summed(LATE_GROUPS, mine, 0), early))
    for stage in (1, 2):
        mine = summed(LATE_GROUPS, mine, stage, early)
    entries = gathered([piece[None] for piece in mine])
    keys = [key for key, _ in entries]
    gram_pieces = [piece.reshape(-1, *piece.shape[-3:]) for _, piece in entries]

    before = None
    for part in range(HALVES):
        slabs = step_call(keys, gram_pieces, own, part)
        if before is not None:
            slabs, before = lax.optimization_barrier((slabs, before))
        got = [home(slabs[step], step) for step in range(4)]
        for step in range(4):
            at = slab_of(high, low, step) * GROUP + part * WIDE
            piece = FACTOR * got[step].reshape(SLAB, WIDE).astype(F32)
            out = lax.dynamic_update_slice_in_dim(out, pick(out, at, WIDE, 1) + piece, at, 1)
        before = got
    return out


def solution(mesh):
    shards = shards_cube if dict(mesh.shape) == {"mats": 2, "col": 4, "row": 4} else shards_rows
    in_specs = (P(("mats", "row"), "col"),)
    out_specs = P(("mats", "row"), "col")
    return jax.shard_map(shards, mesh=mesh, in_specs=in_specs, out_specs=out_specs, check_vma=False)
```

```python
import functools
import math

import jax
import jax.numpy as jnp
from jax import lax
from jax.experimental import pallas as pl
from jax.experimental.pallas import tpu as pltpu
from jax.sharding import PartitionSpec as P

ORDER = 3584
COLS = 8192

BF16 = jnp.bfloat16
F32 = jnp.float32

quint_a = 3.4445
quint_b = -4.775
quint_c = 2.0315

FACTOR = 0.2 * math.sqrt(max(ORDER, COLS))

BLOCK = 512
BLOCKS = ORDER // BLOCK
DIAGS = 4
MINE = DIAGS * BLOCKS // 2
THIRDS = ((0, 5), (5, 10), (10, 14))
PLACES = 8
UNIT = BLOCK // PLACES
TAIL = 16
SLAB = ORDER // 4
BAND = SLAB // BLOCKS
GROUP = COLS // 16
HOPS = (1, 2, 4)
LAST = (2, 2)
PIECES = (3, 4)
HALVES = 2
WIDE = GROUP // HALVES
GRAM_VMEM = 28 << 20
STEP_VMEM = 60 << 20


def shards_rows(iterate):
    iter_bf = iterate.astype(BF16)
    column_panel = lax.all_gather(iter_bf, "row", axis=0, tiled=True)
    gram_part = lax.psum_scatter(
        lax.dot_general(
            column_panel, iter_bf, (((1,), (1,)), ((), ())), preferred_element_type=F32
        ),
        "col",
        scatter_dimension=0,
        tiled=True,
    )
    gram_cols = lax.all_gather(gram_part.astype(BF16), "col", axis=0, tiled=True)
    first = lax.dot_general(
        gram_cols, column_panel, (((0,), (0,)), ((), ())), preferred_element_type=F32
    )
    second = lax.dot_general(
        gram_cols,
        lax.all_gather(first.astype(BF16), "row", axis=0, tiled=True),
        (((0,), (0,)), ((), ())),
        preferred_element_type=F32,
    )
    return FACTOR * (quint_a * iterate + quint_b * first + quint_c * second)


def flip(bit, by):
    return 1 - bit if by else bit


def place():
    col = lax.axis_index("col")
    row = lax.axis_index("row")
    return lax.axis_index("mats"), col // 2, col % 2, row // 2, row % 2


def slab_of(high, low, step):
    return 2 * flip(high, step >> 1) + flip(low, step & 1)


def place_of(x, y, low, by):
    return 4 * flip(x, by >> 2) + 2 * flip(y, by >> 1 & 1) + flip(low, by & 1)


def over_x(a):
    return lax.ppermute(a, "col", [(0, 2), (1, 3), (2, 0), (3, 1)])


def over_core(a):
    return lax.ppermute(a, "col", [(0, 1), (1, 0), (2, 3), (3, 2)])


def over_y(a):
    return lax.ppermute(a, "mats", [(0, 1), (1, 0)])


def over_z(a, step=1):
    return lax.ppermute(a, "row", [(z, z ^ step) for z in range(4)])


MOVES = {4: over_x, 2: over_y, 1: over_z}
ORDERS = ((4, 2, 1), (2, 1, 4), (1, 4, 2))

EARLY = (((0, 0), (1, 0), (2, 0)), ((0, 1), (1, 1), (0, 2)))
LATE = [
    (i, d) for d in range(DIAGS) for i in range(BLOCKS) if (i, d) not in EARLY[0] + EARLY[1]
]
LATE = (LATE[: MINE - 3], LATE[MINE - 3 :])
EARLY_GROUPS = tuple(
    ([core[lo:hi] for core in EARLY], order)
    for (lo, hi), order in (((0, 3), (4, 2, 1)),)
)
LATE_GROUPS = tuple(
    ([core[lo:hi] for core in LATE], order)
    for (lo, hi), order in zip(((0, 4), (4, 8), (8, 11)), ORDERS)
)
SPOT = {
    block: core * MINE + THIRDS[third][0] + n
    for core in range(2)
    for third in range(3)
    for n, block in enumerate([EARLY[core][third]] + LATE_GROUPS[third][0][core])
}


def lookup(index, values):
    got = values[0]
    for n, value in enumerate(values[1:], 1):
        got = jnp.where(index == n, value, got)
    return got


def home(a, step):
    pairs = []
    for y in range(2):
        for z in range(4):
            part, slab = z // 2, (2 * y + z % 2) ^ step
            pairs.append((4 * y + z, 4 * part + slab))
    return lax.ppermute(a, ("mats", "row"), pairs)


def dot(a, b, dims):
    return lax.dot_general(a, b, (dims, ((), ())), preferred_element_type=F32)


def block_rows(p):
    return pl.ds(sum(PIECES[:p]), PIECES[p])


def on_diagonal(unit):
    shape = (UNIT, BLOCK)
    return lax.broadcasted_iota(jnp.int32, shape, 0) + unit * UNIT == lax.broadcasted_iota(
        jnp.int32, shape, 1
    )


def kept(order, stage):
    gone = sum(order[: stage + 1])
    return [by for by in range(PLACES) if not by & gone]


def sent(order, stage):
    return [by | order[stage] for by in kept(order, stage)]


def rows_sent(group, stage):
    blocks, order = group
    return len(blocks[0]) * len(sent(order, stage)) * UNIT


def exchange_shapes(group, stage):
    blocks, order = group
    return [
        jax.ShapeDtypeStruct((len(blocks[0]), len(kept(order, stage)), UNIT, BLOCK), F32),
        jax.ShapeDtypeStruct((rows_sent(group, stage) + TAIL, BLOCK), BF16),
    ]


def write_sent(send, tail, e, parts, units, flag):
    left = jnp.zeros((1, BLOCK), F32)
    for n, (part, unit) in enumerate(zip(parts, units)):
        near = part.astype(BF16)
        row = (e * len(parts) + n) * UNIT
        send[pl.ds(row if isinstance(row, int) else pl.multiple_of(row, UNIT), UNIT), :] = near
        if flag is not None:
            rest = jnp.where(on_diagonal(unit), part - near.astype(F32), 0.0)
            left += jnp.sum(rest, axis=0, keepdims=True)
    if flag is not None:
        tail[pl.ds(e, 1), :] = left * flag


def gram_kernel(groups, pieces, *refs):
    inputs, refs = refs[: 2 * pieces], refs[2 * pieces :]
    count = 2 * len(groups)
    outs, refs = refs[:count], refs[count:]
    keeps, sends, refs = refs[0:count:2], refs[1:count:2], refs[count:]
    tails, (panel, arrived, gone) = refs[: len(groups)], refs[len(groups) :]
    y, x, core, high, low = place()
    for source in range(2):
        for p in range(pieces):
            for step in range(4):
                spot = pl.multiple_of(slab_of(high, low, step) * BAND, BAND)
                columns = pl.ds(source * GROUP, GROUP)
                pltpu.make_async_copy(
                    inputs[source * pieces + p].at[step],
                    panel.at[block_rows(p), pl.ds(spot, BAND), columns],
                    arrived,
                ).start()
    for tail in tails:
        tail[...] = jnp.zeros_like(tail)
    pltpu.make_async_copy(panel, panel, arrived).wait()
    for g, group in enumerate(groups):
        blocks, order = group
        keep, send, tail = keeps[g], sends[g], tails[g]
        size = len(sent(order, 0)) * UNIT
        diagonal = blocks[0][0][1] == 0

        def block(e, carry):
            at = [
                jnp.where(core == 0, lookup(e, [b[n] for b in blocks[0]]), lookup(e, [b[n] for b in blocks[1]]))
                for n in range(2)
            ]
            i, j = at[0], lax.rem(at[0] + at[1], BLOCKS)
            rows = [
                panel[i, pl.ds(pl.multiple_of(place_of(x, y, low, by) * UNIT, UNIT), UNIT), :]
                for by in range(PLACES)
            ]
            got = dot(jnp.concatenate(rows), panel[j], ((1,), (1,)))
            for n, by in enumerate(kept(order, 0)):
                keep[e, n] = got[by * UNIT : (by + 1) * UNIT]
            parts = [got[by * UNIT : (by + 1) * UNIT] for by in sent(order, 0)]
            units = [place_of(x, y, low, by) for by in sent(order, 0)]
            write_sent(send, tail, e, parts, units, (core == 0).astype(F32) if diagonal else None)
            pltpu.make_async_copy(keep.at[e], outs[2 * g].at[e], gone.at[2 * g]).start()
            rows = pl.ds(pl.multiple_of(e * size, size), size)
            pltpu.make_async_copy(
                send.at[rows, :], outs[2 * g + 1].at[rows, :], gone.at[2 * g + 1]
            ).start()
            return carry

        lax.fori_loop(0, len(blocks[0]), block, 0)
        rows = pl.ds(rows_sent(group, 0), TAIL)
        send[rows, :] = tail[...].astype(BF16)
        pltpu.make_async_copy(
            send.at[rows, :], outs[2 * g + 1].at[rows, :], gone.at[2 * g + 1]
        ).start()
    for g in range(len(groups)):
        for n, ref in ((2 * g, keeps[g]), (2 * g + 1, sends[g])):
            pltpu.make_async_copy(ref, outs[n], gone.at[n]).wait()


def add_kernel(groups, stage, before, *refs):
    last = stage == 2
    count = 2 * len(groups)
    keeps, gots, refs = refs[0:count:2], refs[1:count:2], refs[count:]
    early, outs = refs[:before], refs[before:]
    y, x, core, high, low = place()
    for g, group in enumerate(groups):
        blocks, order = group
        keep, got = keeps[g], gots[g]
        held = kept(order, stage)
        diagonal = blocks[0][0][1] == 0
        left = got[pl.ds(rows_sent(group, stage), TAIL), :].astype(F32)
        skip = 0
        if last and before:
            skip = 1
            outs[g][0] = early[0][g]
        if not last:
            nxt, send, tail = outs[2 * g], outs[2 * g + 1], outs[count + g]
            tail[...] = jnp.zeros_like(tail)
        for e in range(len(blocks[0])):
            sums = {}
            for n, by in enumerate(held):
                row = (e * len(held) + n) * UNIT
                here = keep[e, n] + got[row : row + UNIT, :].astype(F32)
                if diagonal:
                    unit = place_of(x, y, low, by)
                    here += jnp.where(on_diagonal(unit), left[e : e + 1, :], 0.0)
                sums[by] = here
            if last:
                outs[g][skip + e] = sums[0].astype(BF16)
                continue
            for n, by in enumerate(kept(order, stage + 1)):
                nxt[e, n] = sums[by]
            going = sent(order, stage + 1)
            units = [place_of(x, y, low, by) for by in going]
            flag = (core == 0).astype(F32) if diagonal else None
            write_sent(send, tail, e, [sums[by] for by in going], units, flag)
        if not last:
            send[pl.ds(rows_sent(group, stage + 1), TAIL), :] = tail[...].astype(BF16)


def gram_call(groups, own, beside):
    inputs = own + beside
    rows = sum(PIECES[: len(own)])
    shapes = [shape for group in groups for shape in exchange_shapes(group, 0)]
    return pl.pallas_call(
        functools.partial(gram_kernel, groups, len(own)),
        out_shape=shapes,
        in_specs=[pl.BlockSpec(memory_space=pl.ANY)] * len(inputs),
        out_specs=[pl.BlockSpec(memory_space=pl.ANY)] * len(shapes),
        scratch_shapes=[pltpu.VMEM(shape.shape, shape.dtype) for shape in shapes]
        + [pltpu.VMEM((TAIL, BLOCK), F32)] * len(groups)
        + [
            pltpu.VMEM((rows, BLOCK, 2 * GROUP), BF16),
            pltpu.SemaphoreType.DMA,
            pltpu.SemaphoreType.DMA((len(shapes),)),
        ],
        compiler_params=pltpu.CompilerParams(vmem_limit_bytes=GRAM_VMEM),
        cost_estimate=pl.CostEstimate(
            flops=len(own) // 2 * MINE * 2 * BLOCK * BLOCK * 2 * GROUP,
            bytes_accessed=rows << 16,
            transcendentals=0,
        ),
        name="gram",
    )(*inputs)


def add_call(groups, stage, inputs, early):
    if stage < 2:
        shapes = [shape for group in groups for shape in exchange_shapes(group, stage + 1)]
        scratch = [pltpu.VMEM((TAIL, BLOCK), F32)] * len(groups)
        early = []
    else:
        extra = 1 if early else 0
        shapes = [
            jax.ShapeDtypeStruct((len(blocks[0]) + extra, UNIT, BLOCK), BF16) for blocks, _ in groups
        ]
        scratch = []
    inputs = inputs + early
    return pl.pallas_call(
        functools.partial(add_kernel, groups, stage, len(early)),
        out_shape=shapes,
        in_specs=[pl.BlockSpec(memory_space=pltpu.VMEM)] * len(inputs),
        out_specs=[pl.BlockSpec(memory_space=pltpu.VMEM)] * len(shapes),
        scratch_shapes=scratch,
        compiler_params=pltpu.CompilerParams(vmem_limit_bytes=40 << 20),
        cost_estimate=pl.CostEstimate(flops=1 << 16, bytes_accessed=1 << 16, transcendentals=0),
        name="add",
    )(*inputs)


def summed(groups, parts, stage, early=(), beside=None):
    inputs = []
    for g, (_, order) in enumerate(groups):
        inputs += [parts[2 * g], MOVES[order[stage]](parts[2 * g + 1])]
    if beside is not None:
        inputs, beside = lax.optimization_barrier((inputs, beside))
        return add_call(groups, stage, inputs, list(early)), beside
    return add_call(groups, stage, inputs, list(early))


def gathered(mine):
    thirds = range(3)

    def move(stage, pieces):
        return [
            ([by ^ ORDERS[t][stage] for by in pieces[t][0]], MOVES[ORDERS[t][stage]](pieces[t][1]))
            for t in thirds
        ]

    def wave(*groups):
        return lax.optimization_barrier(groups)

    out = []

    def place_in(pieces, core):
        out.extend(((t, bys, core), piece) for t, (bys, piece) in enumerate(pieces))

    def across(pieces):
        place_in(pieces, 0)
        place_in([(bys, over_core(piece)) for bys, piece in pieces], 1)

    def merge(a, b):
        return [(p[0] + q[0], jnp.concatenate([p[1], q[1]])) for p, q in zip(a, b)]

    def unkeyed(pieces):
        return [piece for _, piece in pieces]

    def keyed(pieces, arrays):
        return [(bys, array) for (bys, _), array in zip(pieces, arrays)]

    def ordered(*groups):
        done = wave([unkeyed(group) for group in groups], [piece for _, piece in out[:-6]])
        out[:-6] = [(key, piece) for (key, _), piece in zip(out, done[1])]
        return [keyed(group, arrays) for group, arrays in zip(groups, done[0])]

    own = [([0], piece) for piece in mine]
    (pair,) = ordered(merge(own, move(0, own)))
    second = move(1, pair)
    across(pair)
    pair, second = ordered(pair, second)
    third_a = move(2, pair)
    across(second)
    second, third_a = ordered(second, third_a)
    third_b = move(2, second)
    across(third_a)
    across(third_b)
    return out


def step_kernel(keys, part, *refs):
    gram_pieces = refs[: len(keys)]
    refs = refs[len(keys) :]
    iter_pieces = refs[: len(PIECES)]
    outs = refs[len(PIECES) : len(PIECES) + 4]
    gram, panel, first, total, result, here, there, gone = refs[len(PIECES) + 4 :]
    y, x, core, high, low = place()
    for p in range(len(PIECES)):
        for step in range(4):
            pltpu.make_async_copy(
                iter_pieces[p].at[step, :, :, pl.ds(part * WIDE, WIDE)],
                panel.at[block_rows(p), slab_of(high, low, step)],
                there,
            ).start()
    for (third, bys, other), piece in zip(keys, gram_pieces):
        lo, hi = THIRDS[third]
        for n, by in enumerate(bys):
            pltpu.make_async_copy(
                piece.at[n],
                gram.at[
                    pl.ds(flip(core, other) * MINE + lo, hi - lo), place_of(x, y, low, by)
                ],
                here,
            ).start()
    pltpu.make_async_copy(panel, panel, there).wait()
    pltpu.make_async_copy(gram, gram, here).wait()

    def rows_of(i):
        return pl.ds(pl.multiple_of(i * BLOCK, BLOCK), BLOCK)

    def block(d, i):
        return gram[lookup(i, [SPOT[n, d] for n in range(BLOCKS)])].reshape(BLOCK, BLOCK)

    def apply(source, i):
        got = dot(block(0, i), source(i), ((1,), (0,)))
        for d in range(1, DIAGS):
            j = lax.rem(i + d, BLOCKS)
            got += dot(block(d, i), source(j), ((1,), (0,)))
            j = lax.rem(i + BLOCKS - d, BLOCKS)
            got += dot(block(d, j), source(j), ((0,), (0,)))
        return got

    def iter_rows(i):
        return panel[i].reshape(BLOCK, WIDE)

    def one(i, carry):
        got = apply(iter_rows, i)
        first[rows_of(i), :] = got.astype(BF16)
        total[rows_of(i), :] = quint_a * iter_rows(i).astype(F32) + quint_b * got
        return carry

    def two(i, carry):
        got = apply(lambda j: first[rows_of(j), :], i)
        result[i] = (total[rows_of(i), :] + quint_c * got).astype(BF16).reshape(4, BAND, WIDE)
        for step in range(4):
            pltpu.make_async_copy(
                result.at[i, slab_of(y, low, step)], outs[step].at[i], gone.at[step]
            ).start()
        return carry

    lax.fori_loop(0, BLOCKS, one, 0)
    lax.fori_loop(0, BLOCKS, two, 0)
    for step in range(4):
        pltpu.make_async_copy(result.at[:, 0], outs[step], gone.at[step]).wait()


def step_call(keys, gram_pieces, iter_pieces, part):
    count = len(gram_pieces) + len(iter_pieces)
    return pl.pallas_call(
        functools.partial(step_kernel, keys, part),
        out_shape=[jax.ShapeDtypeStruct((BLOCKS, BAND, WIDE), BF16)] * 4,
        in_specs=[pl.BlockSpec(memory_space=pl.ANY)] * count,
        out_specs=[pl.BlockSpec(memory_space=pl.ANY)] * 4,
        scratch_shapes=[
            pltpu.VMEM((2 * MINE, PLACES, UNIT, BLOCK), BF16),
            pltpu.VMEM((BLOCKS, 4, BAND, WIDE), BF16),
            pltpu.VMEM((ORDER, WIDE), BF16),
            pltpu.VMEM((ORDER, WIDE), F32),
            pltpu.VMEM((BLOCKS, 4, BAND, WIDE), BF16),
            pltpu.SemaphoreType.DMA,
            pltpu.SemaphoreType.DMA,
            pltpu.SemaphoreType.DMA((4,)),
        ],
        compiler_params=pltpu.CompilerParams(vmem_limit_bytes=STEP_VMEM),
        cost_estimate=pl.CostEstimate(
            flops=4 * ORDER * ORDER * WIDE, bytes_accessed=20 << 20, transcendentals=0
        ),
        name="step",
    )(*gram_pieces, *iter_pieces)


def pick(a, at, size, axis):
    return lax.dynamic_slice_in_dim(a, at, size, axis)


def panels(iterate):
    y, x, core, high, low = place()
    aligned = y == high
    starts = [sum(HOPS[:n]) * BAND for n in range(len(HOPS))]

    def cast(n, at):
        size = (HOPS[n] * BAND, 2 * GROUP)
        return lax.dynamic_slice(iterate, (starts[n], at * 2 * GROUP), size).astype(BF16)

    def chunks(keep, other):
        near, far = jnp.where(aligned, keep, other), jnp.where(aligned, other, keep)
        return [
            pick(far if step >> 1 else near, flip(low, step & 1) * GROUP, GROUP, 1)
            for step in range(4)
        ]

    def travel(ready):
        return [ready[0]] + [over_z(ready[step], step) for step in (1, 2, 3)]

    def joined(pieces):
        return jnp.stack([jnp.concatenate(slab) for slab in zip(*pieces)]).reshape(4, -1, BAND, GROUP)

    done = []
    keep, other = cast(0, y), over_y(cast(0, 1 - y))
    ahead = [(cast(n, y), cast(n, 1 - y)) for n in range(1, len(HOPS))]
    for n in range(len(HOPS) - 1):
        ready, ahead, done = lax.optimization_barrier((chunks(keep, other), ahead, done))
        done.append(travel(ready))
        keep, other = ahead[n][0], over_y(ahead[n][1])
    ready = chunks(keep, other)
    own = [joined(done)]
    done, parts, start = [], None, 0
    for n, blocks in enumerate(LAST):
        stop = start + blocks * BAND
        now, ready, done, own, parts = lax.optimization_barrier(
            ([chunk[start:stop] for chunk in ready], ready, done, own, parts)
        )
        start = stop
        done.append(travel(now))
        if n == 0:
            beside = [over_core(own[0])]
            parts = gram_call(EARLY_GROUPS, own, beside)
        else:
            parts = summed(EARLY_GROUPS, parts, n - 1)
    out = (FACTOR * quint_a) * (iterate - lax.reduce_precision(iterate, 8, 7))
    out, parts, done = lax.optimization_barrier((out, parts, done))
    own.append(joined(done))
    beside.append(over_core(own[1]))
    return own, beside, parts, out


def shards_cube(iterate):
    y, x, core, high, low = place()
    own, beside, early, out = panels(iterate)
    early, mine = summed(EARLY_GROUPS, early, 1, beside=gram_call(LATE_GROUPS, own, beside))
    early = summed(EARLY_GROUPS, early, 2)
    mine, early = lax.optimization_barrier((summed(LATE_GROUPS, mine, 0), early))
    for stage in (1, 2):
        mine = summed(LATE_GROUPS, mine, stage, early)
    entries = gathered([piece[None] for piece in mine])
    keys = [key for key, _ in entries]
    gram_pieces = [piece.reshape(-1, *piece.shape[-3:]) for _, piece in entries]

    before = None
    for part in range(HALVES):
        slabs = step_call(keys, gram_pieces, own, part)
        if before is not None:
            slabs, before = lax.optimization_barrier((slabs, before))
        got = [home(slabs[step], step) for step in range(4)]
        for step in range(4):
            at = slab_of(high, low, step) * GROUP + part * WIDE
            piece = FACTOR * got[step].reshape(SLAB, WIDE).astype(F32)
            out = lax.dynamic_update_slice_in_dim(out, pick(out, at, WIDE, 1) + piece, at, 1)
        before = got
    return out


def solution(mesh):
    shards = shards_cube if dict(mesh.shape) == {"mats": 2, "col": 4, "row": 4} else shards_rows
    in_specs = (P(("mats", "row"), "col"),)
    out_specs = P(("mats", "row"), "col")
    return jax.shard_map(shards, mesh=mesh, in_specs=in_specs, out_specs=out_specs, check_vma=False)
```

```python
import functools
import math

import jax
import jax.numpy as jnp
from jax import lax
from jax.experimental import pallas as pl
from jax.experimental.pallas import tpu as pltpu
from jax.sharding import PartitionSpec as P

ORDER = 3584
COLS = 8192

BF16 = jnp.bfloat16
F32 = jnp.float32

quint_a = 3.4445
quint_b = -4.775
quint_c = 2.0315

FACTOR = 0.2 * math.sqrt(max(ORDER, COLS))

BLOCK = 512
BLOCKS = ORDER // BLOCK
DIAGS = 4
MINE = DIAGS * BLOCKS // 2
THIRDS = ((0, 5), (5, 10), (10, 14))
PLACES = 8
UNIT = BLOCK // PLACES
TAIL = 16
SLAB = ORDER // 4
BAND = SLAB // BLOCKS
GROUP = COLS // 16
HOPS = (1, 2, 4)
LAST = (2, 2)
PIECES = (3, 2, 2)
HALVES = 2
WIDE = GROUP // HALVES
GRAM_VMEM = 28 << 20
STEP_VMEM = 60 << 20


def shards_rows(iterate):
    iter_bf = iterate.astype(BF16)
    column_panel = lax.all_gather(iter_bf, "row", axis=0, tiled=True)
    gram_part = lax.psum_scatter(
        lax.dot_general(
            column_panel, iter_bf, (((1,), (1,)), ((), ())), preferred_element_type=F32
        ),
        "col",
        scatter_dimension=0,
        tiled=True,
    )
    gram_cols = lax.all_gather(gram_part.astype(BF16), "col", axis=0, tiled=True)
    first = lax.dot_general(
        gram_cols, column_panel, (((0,), (0,)), ((), ())), preferred_element_type=F32
    )
    second = lax.dot_general(
        gram_cols,
        lax.all_gather(first.astype(BF16), "row", axis=0, tiled=True),
        (((0,), (0,)), ((), ())),
        preferred_element_type=F32,
    )
    return FACTOR * (quint_a * iterate + quint_b * first + quint_c * second)


def flip(bit, by):
    return 1 - bit if by else bit


def place():
    col = lax.axis_index("col")
    row = lax.axis_index("row")
    return lax.axis_index("mats"), col // 2, col % 2, row // 2, row % 2


def slab_of(high, low, step):
    return 2 * flip(high, step >> 1) + flip(low, step & 1)


def place_of(x, y, low, by):
    return 4 * flip(x, by >> 2) + 2 * flip(y, by >> 1 & 1) + flip(low, by & 1)


def over_x(a):
    return lax.ppermute(a, "col", [(0, 2), (1, 3), (2, 0), (3, 1)])


def over_core(a):
    return lax.ppermute(a, "col", [(0, 1), (1, 0), (2, 3), (3, 2)])


def over_y(a):
    return lax.ppermute(a, "mats", [(0, 1), (1, 0)])


def over_z(a, step=1):
    return lax.ppermute(a, "row", [(z, z ^ step) for z in range(4)])


MOVES = {4: over_x, 2: over_y, 1: over_z}
ORDERS = ((4, 2, 1), (2, 1, 4), (1, 4, 2))

EARLY = (((0, 0), (1, 0), (2, 0)), ((0, 1), (1, 1), (0, 2)))
LATE = [
    (i, d) for d in range(DIAGS) for i in range(BLOCKS) if (i, d) not in EARLY[0] + EARLY[1]
]
LATE = (LATE[: MINE - 3], LATE[MINE - 3 :])
EARLY_GROUPS = tuple(
    ([core[lo:hi] for core in EARLY], order)
    for (lo, hi), order in (((0, 3), (4, 2, 1)),)
)
LATE_GROUPS = tuple(
    ([core[lo:hi] for core in LATE], order)
    for (lo, hi), order in zip(((0, 4), (4, 8), (8, 11)), ORDERS)
)
SPOT = {
    block: core * MINE + THIRDS[third][0] + n
    for core in range(2)
    for third in range(3)
    for n, block in enumerate([EARLY[core][third]] + LATE_GROUPS[third][0][core])
}


def lookup(index, values):
    got = values[0]
    for n, value in enumerate(values[1:], 1):
        got = jnp.where(index == n, value, got)
    return got


def home(a, step):
    pairs = []
    for y in range(2):
        for z in range(4):
            part, slab = z // 2, (2 * y + z % 2) ^ step
            pairs.append((4 * y + z, 4 * part + slab))
    return lax.ppermute(a, ("mats", "row"), pairs)


def dot(a, b, dims):
    return lax.dot_general(a, b, (dims, ((), ())), preferred_element_type=F32)


def block_rows(p):
    return pl.ds(sum(PIECES[:p]), PIECES[p])


def on_diagonal(unit):
    shape = (UNIT, BLOCK)
    return lax.broadcasted_iota(jnp.int32, shape, 0) + unit * UNIT == lax.broadcasted_iota(
        jnp.int32, shape, 1
    )


def kept(order, stage):
    gone = sum(order[: stage + 1])
    return [by for by in range(PLACES) if not by & gone]


def sent(order, stage):
    return [by | order[stage] for by in kept(order, stage)]


def rows_sent(group, stage):
    blocks, order = group
    return len(blocks[0]) * len(sent(order, stage)) * UNIT


def exchange_shapes(group, stage):
    blocks, order = group
    return [
        jax.ShapeDtypeStruct((len(blocks[0]), len(kept(order, stage)), UNIT, BLOCK), F32),
        jax.ShapeDtypeStruct((rows_sent(group, stage) + TAIL, BLOCK), BF16),
    ]


def write_sent(send, tail, e, parts, units, flag):
    left = jnp.zeros((1, BLOCK), F32)
    for n, (part, unit) in enumerate(zip(parts, units)):
        near = part.astype(BF16)
        row = (e * len(parts) + n) * UNIT
        send[pl.ds(row if isinstance(row, int) else pl.multiple_of(row, UNIT), UNIT), :] = near
        if flag is not None:
            rest = jnp.where(on_diagonal(unit), part - near.astype(F32), 0.0)
            left += jnp.sum(rest, axis=0, keepdims=True)
    if flag is not None:
        tail[pl.ds(e, 1), :] = left * flag


def gram_kernel(groups, pieces, *refs):
    inputs, refs = refs[: 2 * pieces], refs[2 * pieces :]
    count = 2 * len(groups)
    outs, refs = refs[:count], refs[count:]
    keeps, sends, refs = refs[0:count:2], refs[1:count:2], refs[count:]
    tails, (panel, arrived, gone) = refs[: len(groups)], refs[len(groups) :]
    y, x, core, high, low = place()
    for source in range(2):
        for p in range(pieces):
            for step in range(4):
                spot = pl.multiple_of(slab_of(high, low, step) * BAND, BAND)
                columns = pl.ds(source * GROUP, GROUP)
                pltpu.make_async_copy(
                    inputs[source * pieces + p].at[step],
                    panel.at[block_rows(p), pl.ds(spot, BAND), columns],
                    arrived,
                ).start()
    for tail in tails:
        tail[...] = jnp.zeros_like(tail)
    pltpu.make_async_copy(panel, panel, arrived).wait()
    for g, group in enumerate(groups):
        blocks, order = group
        keep, send, tail = keeps[g], sends[g], tails[g]
        size = len(sent(order, 0)) * UNIT
        diagonal = blocks[0][0][1] == 0

        def block(e, carry):
            at = [
                jnp.where(core == 0, lookup(e, [b[n] for b in blocks[0]]), lookup(e, [b[n] for b in blocks[1]]))
                for n in range(2)
            ]
            i, j = at[0], lax.rem(at[0] + at[1], BLOCKS)
            rows = [
                panel[i, pl.ds(pl.multiple_of(place_of(x, y, low, by) * UNIT, UNIT), UNIT), :]
                for by in range(PLACES)
            ]
            got = dot(jnp.concatenate(rows), panel[j], ((1,), (1,)))
            for n, by in enumerate(kept(order, 0)):
                keep[e, n] = got[by * UNIT : (by + 1) * UNIT]
            parts = [got[by * UNIT : (by + 1) * UNIT] for by in sent(order, 0)]
            units = [place_of(x, y, low, by) for by in sent(order, 0)]
            write_sent(send, tail, e, parts, units, (core == 0).astype(F32) if diagonal else None)
            pltpu.make_async_copy(keep.at[e], outs[2 * g].at[e], gone.at[2 * g]).start()
            rows = pl.ds(pl.multiple_of(e * size, size), size)
            pltpu.make_async_copy(
                send.at[rows, :], outs[2 * g + 1].at[rows, :], gone.at[2 * g + 1]
            ).start()
            return carry

        lax.fori_loop(0, len(blocks[0]), block, 0)
        rows = pl.ds(rows_sent(group, 0), TAIL)
        send[rows, :] = tail[...].astype(BF16)
        pltpu.make_async_copy(
            send.at[rows, :], outs[2 * g + 1].at[rows, :], gone.at[2 * g + 1]
        ).start()
    for g in range(len(groups)):
        for n, ref in ((2 * g, keeps[g]), (2 * g + 1, sends[g])):
            pltpu.make_async_copy(ref, outs[n], gone.at[n]).wait()


def add_kernel(groups, stage, before, *refs):
    last = stage == 2
    count = 2 * len(groups)
    keeps, gots, refs = refs[0:count:2], refs[1:count:2], refs[count:]
    early, outs = refs[:before], refs[before:]
    y, x, core, high, low = place()
    for g, group in enumerate(groups):
        blocks, order = group
        keep, got = keeps[g], gots[g]
        held = kept(order, stage)
        diagonal = blocks[0][0][1] == 0
        left = got[pl.ds(rows_sent(group, stage), TAIL), :].astype(F32)
        skip = 0
        if last and before:
            skip = 1
            outs[g][0] = early[0][g]
        if not last:
            nxt, send, tail = outs[2 * g], outs[2 * g + 1], outs[count + g]
            tail[...] = jnp.zeros_like(tail)
        for e in range(len(blocks[0])):
            sums = {}
            for n, by in enumerate(held):
                row = (e * len(held) + n) * UNIT
                here = keep[e, n] + got[row : row + UNIT, :].astype(F32)
                if diagonal:
                    unit = place_of(x, y, low, by)
                    here += jnp.where(on_diagonal(unit), left[e : e + 1, :], 0.0)
                sums[by] = here
            if last:
                outs[g][skip + e] = sums[0].astype(BF16)
                continue
            for n, by in enumerate(kept(order, stage + 1)):
                nxt[e, n] = sums[by]
            going = sent(order, stage + 1)
            units = [place_of(x, y, low, by) for by in going]
            flag = (core == 0).astype(F32) if diagonal else None
            write_sent(send, tail, e, [sums[by] for by in going], units, flag)
        if not last:
            send[pl.ds(rows_sent(group, stage + 1), TAIL), :] = tail[...].astype(BF16)


def gram_call(groups, own, beside):
    inputs = own + beside
    rows = sum(PIECES[: len(own)])
    shapes = [shape for group in groups for shape in exchange_shapes(group, 0)]
    return pl.pallas_call(
        functools.partial(gram_kernel, groups, len(own)),
        out_shape=shapes,
        in_specs=[pl.BlockSpec(memory_space=pl.ANY)] * len(inputs),
        out_specs=[pl.BlockSpec(memory_space=pl.ANY)] * len(shapes),
        scratch_shapes=[pltpu.VMEM(shape.shape, shape.dtype) for shape in shapes]
        + [pltpu.VMEM((TAIL, BLOCK), F32)] * len(groups)
        + [
            pltpu.VMEM((rows, BLOCK, 2 * GROUP), BF16),
            pltpu.SemaphoreType.DMA,
            pltpu.SemaphoreType.DMA((len(shapes),)),
        ],
        compiler_params=pltpu.CompilerParams(vmem_limit_bytes=GRAM_VMEM),
        cost_estimate=pl.CostEstimate(
            flops=len(own) // 2 * MINE * 2 * BLOCK * BLOCK * 2 * GROUP,
            bytes_accessed=rows << 16,
            transcendentals=0,
        ),
        name="gram",
    )(*inputs)


def add_call(groups, stage, inputs, early):
    if stage < 2:
        shapes = [shape for group in groups for shape in exchange_shapes(group, stage + 1)]
        scratch = [pltpu.VMEM((TAIL, BLOCK), F32)] * len(groups)
        early = []
    else:
        extra = 1 if early else 0
        shapes = [
            jax.ShapeDtypeStruct((len(blocks[0]) + extra, UNIT, BLOCK), BF16) for blocks, _ in groups
        ]
        scratch = []
    inputs = inputs + early
    return pl.pallas_call(
        functools.partial(add_kernel, groups, stage, len(early)),
        out_shape=shapes,
        in_specs=[pl.BlockSpec(memory_space=pltpu.VMEM)] * len(inputs),
        out_specs=[pl.BlockSpec(memory_space=pltpu.VMEM)] * len(shapes),
        scratch_shapes=scratch,
        compiler_params=pltpu.CompilerParams(vmem_limit_bytes=40 << 20),
        cost_estimate=pl.CostEstimate(flops=1 << 16, bytes_accessed=1 << 16, transcendentals=0),
        name="add",
    )(*inputs)


def summed(groups, parts, stage, early=(), beside=None):
    inputs = []
    for g, (_, order) in enumerate(groups):
        inputs += [parts[2 * g], MOVES[order[stage]](parts[2 * g + 1])]
    if beside is not None:
        inputs, beside = lax.optimization_barrier((inputs, beside))
        return add_call(groups, stage, inputs, list(early)), beside
    return add_call(groups, stage, inputs, list(early))


def gathered(mine):
    thirds = range(3)

    def move(stage, pieces):
        return [
            ([by ^ ORDERS[t][stage] for by in pieces[t][0]], MOVES[ORDERS[t][stage]](pieces[t][1]))
            for t in thirds
        ]

    def wave(*groups):
        return lax.optimization_barrier(groups)

    out = []

    def place_in(pieces, core):
        out.extend(((t, bys, core), piece) for t, (bys, piece) in enumerate(pieces))

    def across(pieces):
        place_in(pieces, 0)
        place_in([(bys, over_core(piece)) for bys, piece in pieces], 1)

    def merge(a, b):
        return [(p[0] + q[0], jnp.concatenate([p[1], q[1]])) for p, q in zip(a, b)]

    def unkeyed(pieces):
        return [piece for _, piece in pieces]

    def keyed(pieces, arrays):
        return [(bys, array) for (bys, _), array in zip(pieces, arrays)]

    def ordered(*groups):
        done = wave([unkeyed(group) for group in groups], [piece for _, piece in out[:-6]])
        out[:-6] = [(key, piece) for (key, _), piece in zip(out, done[1])]
        return [keyed(group, arrays) for group, arrays in zip(groups, done[0])]

    own = [([0], piece) for piece in mine]
    pair = merge(own, move(0, own))
    second = move(1, pair)
    across(pair)
    pair, second = ordered(pair, second)
    third_a = move(2, pair)
    across(second)
    second, third_a = ordered(second, third_a)
    third_b = move(2, second)
    across(third_a)
    across(third_b)
    return out


def step_kernel(keys, part, *refs):
    gram_pieces = refs[: len(keys)]
    refs = refs[len(keys) :]
    iter_pieces = refs[: len(PIECES)]
    outs = refs[len(PIECES) : len(PIECES) + 4]
    gram, panel, first, total, result, here, there, gone = refs[len(PIECES) + 4 :]
    y, x, core, high, low = place()
    for p in range(len(PIECES)):
        for step in range(4):
            pltpu.make_async_copy(
                iter_pieces[p].at[step, :, :, pl.ds(part * WIDE, WIDE)],
                panel.at[block_rows(p), slab_of(high, low, step)],
                there,
            ).start()
    for (third, bys, other), piece in zip(keys, gram_pieces):
        lo, hi = THIRDS[third]
        for n, by in enumerate(bys):
            pltpu.make_async_copy(
                piece.at[n],
                gram.at[
                    pl.ds(flip(core, other) * MINE + lo, hi - lo), place_of(x, y, low, by)
                ],
                here,
            ).start()
    pltpu.make_async_copy(panel, panel, there).wait()
    pltpu.make_async_copy(gram, gram, here).wait()

    def rows_of(i):
        return pl.ds(pl.multiple_of(i * BLOCK, BLOCK), BLOCK)

    def block(d, i):
        return gram[lookup(i, [SPOT[n, d] for n in range(BLOCKS)])].reshape(BLOCK, BLOCK)

    def apply(source, i):
        got = dot(block(0, i), source(i), ((1,), (0,)))
        for d in range(1, DIAGS):
            j = lax.rem(i + d, BLOCKS)
            got += dot(block(d, i), source(j), ((1,), (0,)))
            j = lax.rem(i + BLOCKS - d, BLOCKS)
            got += dot(block(d, j), source(j), ((0,), (0,)))
        return got

    def iter_rows(i):
        return panel[i].reshape(BLOCK, WIDE)

    def one(i, carry):
        got = apply(iter_rows, i)
        first[rows_of(i), :] = got.astype(BF16)
        total[rows_of(i), :] = quint_a * iter_rows(i).astype(F32) + quint_b * got
        return carry

    def two(i, carry):
        got = apply(lambda j: first[rows_of(j), :], i)
        result[i] = (total[rows_of(i), :] + quint_c * got).astype(BF16).reshape(4, BAND, WIDE)
        for step in range(4):
            pltpu.make_async_copy(
                result.at[i, slab_of(y, low, step)], outs[step].at[i], gone.at[step]
            ).start()
        return carry

    lax.fori_loop(0, BLOCKS, one, 0)
    lax.fori_loop(0, BLOCKS, two, 0)
    for step in range(4):
        pltpu.make_async_copy(result.at[:, 0], outs[step], gone.at[step]).wait()


def step_call(keys, gram_pieces, iter_pieces, part):
    count = len(gram_pieces) + len(iter_pieces)
    return pl.pallas_call(
        functools.partial(step_kernel, keys, part),
        out_shape=[jax.ShapeDtypeStruct((BLOCKS, BAND, WIDE), BF16)] * 4,
        in_specs=[pl.BlockSpec(memory_space=pl.ANY)] * count,
        out_specs=[pl.BlockSpec(memory_space=pl.ANY)] * 4,
        scratch_shapes=[
            pltpu.VMEM((2 * MINE, PLACES, UNIT, BLOCK), BF16),
            pltpu.VMEM((BLOCKS, 4, BAND, WIDE), BF16),
            pltpu.VMEM((ORDER, WIDE), BF16),
            pltpu.VMEM((ORDER, WIDE), F32),
            pltpu.VMEM((BLOCKS, 4, BAND, WIDE), BF16),
            pltpu.SemaphoreType.DMA,
            pltpu.SemaphoreType.DMA,
            pltpu.SemaphoreType.DMA((4,)),
        ],
        compiler_params=pltpu.CompilerParams(vmem_limit_bytes=STEP_VMEM),
        cost_estimate=pl.CostEstimate(
            flops=4 * ORDER * ORDER * WIDE, bytes_accessed=20 << 20, transcendentals=0
        ),
        name="step",
    )(*gram_pieces, *iter_pieces)


def pick(a, at, size, axis):
    return lax.dynamic_slice_in_dim(a, at, size, axis)


def panels(iterate):
    y, x, core, high, low = place()
    aligned = y == high
    starts = [sum(HOPS[:n]) * BAND for n in range(len(HOPS))]

    def cast(n, at):
        size = (HOPS[n] * BAND, 2 * GROUP)
        return lax.dynamic_slice(iterate, (starts[n], at * 2 * GROUP), size).astype(BF16)

    def chunks(keep, other):
        near, far = jnp.where(aligned, keep, other), jnp.where(aligned, other, keep)
        return [
            pick(far if step >> 1 else near, flip(low, step & 1) * GROUP, GROUP, 1)
            for step in range(4)
        ]

    def travel(ready):
        return [ready[0]] + [over_z(ready[step], step) for step in (1, 2, 3)]

    def joined(pieces):
        return jnp.stack([jnp.concatenate(slab) for slab in zip(*pieces)]).reshape(4, -1, BAND, GROUP)

    done = []
    keep, other = cast(0, y), over_y(cast(0, 1 - y))
    ahead = [(cast(n, y), cast(n, 1 - y)) for n in range(1, len(HOPS))]
    for n in range(len(HOPS) - 1):
        ready, ahead, done = lax.optimization_barrier((chunks(keep, other), ahead, done))
        done.append(travel(ready))
        keep, other = ahead[n][0], over_y(ahead[n][1])
    ready = chunks(keep, other)
    own = [joined(done)]
    done, parts, start = [], None, 0
    for n, blocks in enumerate(LAST):
        stop = start + blocks * BAND
        now, ready, done, own, parts = lax.optimization_barrier(
            ([chunk[start:stop] for chunk in ready], ready, done, own, parts)
        )
        start = stop
        done.append(travel(now))
        if n == 0:
            beside = [over_core(own[0])]
            parts = gram_call(EARLY_GROUPS, own, beside)
        else:
            parts = summed(EARLY_GROUPS, parts, n - 1)
            own.append(joined(done[:1]))
            beside.append(over_core(own[1]))
    out = (FACTOR * quint_a) * (iterate - lax.reduce_precision(iterate, 8, 7))
    out, parts, done = lax.optimization_barrier((out, parts, done))
    own.append(joined(done[1:]))
    beside.append(over_core(own[2]))
    return own, beside, parts, out


def shards_cube(iterate):
    y, x, core, high, low = place()
    own, beside, early, out = panels(iterate)
    early, mine = summed(EARLY_GROUPS, early, 1, beside=gram_call(LATE_GROUPS, own, beside))
    early = summed(EARLY_GROUPS, early, 2)
    mine, early = lax.optimization_barrier((summed(LATE_GROUPS, mine, 0), early))
    for stage in (1, 2):
        mine = summed(LATE_GROUPS, mine, stage, early)
    entries = gathered([piece[None] for piece in mine])
    keys = [key for key, _ in entries]
    gram_pieces = [piece.reshape(-1, *piece.shape[-3:]) for _, piece in entries]

    before = None
    for part in range(HALVES):
        slabs = step_call(keys, gram_pieces, own, part)
        if before is not None:
            slabs, before = lax.optimization_barrier((slabs, before))
        got = [home(slabs[step], step) for step in range(4)]
        for step in range(4):
            at = slab_of(high, low, step) * GROUP + part * WIDE
            piece = FACTOR * got[step].reshape(SLAB, WIDE).astype(F32)
            out = lax.dynamic_update_slice_in_dim(out, pick(out, at, WIDE, 1) + piece, at, 1)
        before = got
    return out


def solution(mesh):
    shards = shards_cube if dict(mesh.shape) == {"mats": 2, "col": 4, "row": 4} else shards_rows
    in_specs = (P(("mats", "row"), "col"),)
    out_specs = P(("mats", "row"), "col")
    return jax.shard_map(shards, mesh=mesh, in_specs=in_specs, out_specs=out_specs, check_vma=False)
```

```python
import functools
import math

import jax
import jax.numpy as jnp
from jax import lax
from jax.experimental import pallas as pl
from jax.experimental.pallas import tpu as pltpu
from jax.sharding import PartitionSpec as P

ORDER = 3584
COLS = 8192

BF16 = jnp.bfloat16
F32 = jnp.float32

quint_a = 3.4445
quint_b = -4.775
quint_c = 2.0315

FACTOR = 0.2 * math.sqrt(max(ORDER, COLS))

BLOCK = 512
BLOCKS = ORDER // BLOCK
DIAGS = 4
MINE = DIAGS * BLOCKS // 2
THIRDS = ((0, 5), (5, 10), (10, 14))
PLACES = 8
UNIT = BLOCK // PLACES
TAIL = 16
SLAB = ORDER // 4
BAND = SLAB // BLOCKS
GROUP = COLS // 16
HOPS = (1, 2, 4)
LAST = (2, 2)
PIECES = (3, 2, 2)
HALVES = 2
WIDE = GROUP // HALVES
GRAM_VMEM = 28 << 20
STEP_VMEM = 60 << 20


def shards_rows(iterate):
    iter_bf = iterate.astype(BF16)
    column_panel = lax.all_gather(iter_bf, "row", axis=0, tiled=True)
    gram_part = lax.psum_scatter(
        lax.dot_general(
            column_panel, iter_bf, (((1,), (1,)), ((), ())), preferred_element_type=F32
        ),
        "col",
        scatter_dimension=0,
        tiled=True,
    )
    gram_cols = lax.all_gather(gram_part.astype(BF16), "col", axis=0, tiled=True)
    first = lax.dot_general(
        gram_cols, column_panel, (((0,), (0,)), ((), ())), preferred_element_type=F32
    )
    second = lax.dot_general(
        gram_cols,
        lax.all_gather(first.astype(BF16), "row", axis=0, tiled=True),
        (((0,), (0,)), ((), ())),
        preferred_element_type=F32,
    )
    return FACTOR * (quint_a * iterate + quint_b * first + quint_c * second)


def flip(bit, by):
    return 1 - bit if by else bit


def place():
    col = lax.axis_index("col")
    row = lax.axis_index("row")
    return lax.axis_index("mats"), col // 2, col % 2, row // 2, row % 2


def slab_of(high, low, step):
    return 2 * flip(high, step >> 1) + flip(low, step & 1)


def place_of(x, y, low, by):
    return 4 * flip(x, by >> 2) + 2 * flip(y, by >> 1 & 1) + flip(low, by & 1)


def over_x(a):
    return lax.ppermute(a, "col", [(0, 2), (1, 3), (2, 0), (3, 1)])


def over_core(a):
    return lax.ppermute(a, "col", [(0, 1), (1, 0), (2, 3), (3, 2)])


def over_y(a):
    return lax.ppermute(a, "mats", [(0, 1), (1, 0)])


def over_z(a, step=1):
    return lax.ppermute(a, "row", [(z, z ^ step) for z in range(4)])


MOVES = {4: over_x, 2: over_y, 1: over_z}
ORDERS = ((4, 2, 1), (2, 1, 4), (1, 4, 2))

EARLY = (((0, 0), (1, 0), (2, 0)), ((0, 1), (1, 1), (0, 2)))
LATE = [
    (i, d) for d in range(DIAGS) for i in range(BLOCKS) if (i, d) not in EARLY[0] + EARLY[1]
]
LATE = (LATE[: MINE - 3], LATE[MINE - 3 :])
EARLY_GROUPS = tuple(
    ([core[lo:hi] for core in EARLY], order)
    for (lo, hi), order in (((0, 3), (4, 2, 1)),)
)
LATE_GROUPS = tuple(
    ([core[lo:hi] for core in LATE], order)
    for (lo, hi), order in zip(((0, 4), (4, 8), (8, 11)), ORDERS)
)
SPOT = {
    block: core * MINE + THIRDS[third][0] + n
    for core in range(2)
    for third in range(3)
    for n, block in enumerate([EARLY[core][third]] + LATE_GROUPS[third][0][core])
}


def lookup(index, values):
    got = values[0]
    for n, value in enumerate(values[1:], 1):
        got = jnp.where(index == n, value, got)
    return got


def home(a, step):
    pairs = []
    for y in range(2):
        for z in range(4):
            part, slab = z // 2, (2 * y + z % 2) ^ step
            pairs.append((4 * y + z, 4 * part + slab))
    return lax.ppermute(a, ("mats", "row"), pairs)


def dot(a, b, dims):
    return lax.dot_general(a, b, (dims, ((), ())), preferred_element_type=F32)


def block_rows(p):
    return pl.ds(sum(PIECES[:p]), PIECES[p])


def on_diagonal(unit):
    shape = (UNIT, BLOCK)
    return lax.broadcasted_iota(jnp.int32, shape, 0) + unit * UNIT == lax.broadcasted_iota(
        jnp.int32, shape, 1
    )


def kept(order, stage):
    gone = sum(order[: stage + 1])
    return [by for by in range(PLACES) if not by & gone]


def sent(order, stage):
    return [by | order[stage] for by in kept(order, stage)]


def rows_sent(group, stage):
    blocks, order = group
    return len(blocks[0]) * len(sent(order, stage)) * UNIT


def exchange_shapes(group, stage):
    blocks, order = group
    return [
        jax.ShapeDtypeStruct((len(blocks[0]), len(kept(order, stage)), UNIT, BLOCK), F32),
        jax.ShapeDtypeStruct((rows_sent(group, stage) + TAIL, BLOCK), BF16),
    ]


def write_sent(send, tail, e, parts, units, flag):
    left = jnp.zeros((1, BLOCK), F32)
    for n, (part, unit) in enumerate(zip(parts, units)):
        near = part.astype(BF16)
        row = (e * len(parts) + n) * UNIT
        send[pl.ds(row if isinstance(row, int) else pl.multiple_of(row, UNIT), UNIT), :] = near
        if flag is not None:
            rest = jnp.where(on_diagonal(unit), part - near.astype(F32), 0.0)
            left += jnp.sum(rest, axis=0, keepdims=True)
    if flag is not None:
        tail[pl.ds(e, 1), :] = left * flag


def gram_kernel(groups, pieces, *refs):
    inputs, refs = refs[: 2 * pieces], refs[2 * pieces :]
    count = 2 * len(groups)
    outs, refs = refs[:count], refs[count:]
    keeps, sends, refs = refs[0:count:2], refs[1:count:2], refs[count:]
    tails, (panel, arrived, gone) = refs[: len(groups)], refs[len(groups) :]
    y, x, core, high, low = place()
    for source in range(2):
        for p in range(pieces):
            for step in range(4):
                spot = pl.multiple_of(slab_of(high, low, step) * BAND, BAND)
                columns = pl.ds(source * GROUP, GROUP)
                pltpu.make_async_copy(
                    inputs[source * pieces + p].at[step],
                    panel.at[block_rows(p), pl.ds(spot, BAND), columns],
                    arrived,
                ).start()
    for tail in tails:
        tail[...] = jnp.zeros_like(tail)
    pltpu.make_async_copy(panel, panel, arrived).wait()
    for g, group in enumerate(groups):
        blocks, order = group
        keep, send, tail = keeps[g], sends[g], tails[g]
        size = len(sent(order, 0)) * UNIT
        diagonal = blocks[0][0][1] == 0

        def block(e, carry):
            at = [
                jnp.where(core == 0, lookup(e, [b[n] for b in blocks[0]]), lookup(e, [b[n] for b in blocks[1]]))
                for n in range(2)
            ]
            i, j = at[0], lax.rem(at[0] + at[1], BLOCKS)
            rows = [
                panel[i, pl.ds(pl.multiple_of(place_of(x, y, low, by) * UNIT, UNIT), UNIT), :]
                for by in range(PLACES)
            ]
            got = dot(jnp.concatenate(rows), panel[j], ((1,), (1,)))
            for n, by in enumerate(kept(order, 0)):
                keep[e, n] = got[by * UNIT : (by + 1) * UNIT]
            parts = [got[by * UNIT : (by + 1) * UNIT] for by in sent(order, 0)]
            units = [place_of(x, y, low, by) for by in sent(order, 0)]
            write_sent(send, tail, e, parts, units, (core == 0).astype(F32) if diagonal else None)
            pltpu.make_async_copy(keep.at[e], outs[2 * g].at[e], gone.at[2 * g]).start()
            rows = pl.ds(pl.multiple_of(e * size, size), size)
            pltpu.make_async_copy(
                send.at[rows, :], outs[2 * g + 1].at[rows, :], gone.at[2 * g + 1]
            ).start()
            return carry

        lax.fori_loop(0, len(blocks[0]), block, 0)
        rows = pl.ds(rows_sent(group, 0), TAIL)
        send[rows, :] = tail[...].astype(BF16)
        pltpu.make_async_copy(
            send.at[rows, :], outs[2 * g + 1].at[rows, :], gone.at[2 * g + 1]
        ).start()
    for g in range(len(groups)):
        for n, ref in ((2 * g, keeps[g]), (2 * g + 1, sends[g])):
            pltpu.make_async_copy(ref, outs[n], gone.at[n]).wait()


def add_kernel(groups, stage, before, *refs):
    last = stage == 2
    count = 2 * len(groups)
    keeps, gots, refs = refs[0:count:2], refs[1:count:2], refs[count:]
    early, outs = refs[:before], refs[before:]
    y, x, core, high, low = place()
    for g, group in enumerate(groups):
        blocks, order = group
        keep, got = keeps[g], gots[g]
        held = kept(order, stage)
        diagonal = blocks[0][0][1] == 0
        left = got[pl.ds(rows_sent(group, stage), TAIL), :].astype(F32)
        skip = 0
        if last and before:
            skip = 1
            outs[g][0] = early[0][g]
        if not last:
            nxt, send, tail = outs[2 * g], outs[2 * g + 1], outs[count + g]
            tail[...] = jnp.zeros_like(tail)
        for e in range(len(blocks[0])):
            sums = {}
            for n, by in enumerate(held):
                row = (e * len(held) + n) * UNIT
                here = keep[e, n] + got[row : row + UNIT, :].astype(F32)
                if diagonal:
                    unit = place_of(x, y, low, by)
                    here += jnp.where(on_diagonal(unit), left[e : e + 1, :], 0.0)
                sums[by] = here
            if last:
                outs[g][skip + e] = sums[0].astype(BF16)
                continue
            for n, by in enumerate(kept(order, stage + 1)):
                nxt[e, n] = sums[by]
            going = sent(order, stage + 1)
            units = [place_of(x, y, low, by) for by in going]
            flag = (core == 0).astype(F32) if diagonal else None
            write_sent(send, tail, e, [sums[by] for by in going], units, flag)
        if not last:
            send[pl.ds(rows_sent(group, stage + 1), TAIL), :] = tail[...].astype(BF16)


def gram_call(groups, own, beside):
    inputs = own + beside
    rows = sum(PIECES[: len(own)])
    shapes = [shape for group in groups for shape in exchange_shapes(group, 0)]
    return pl.pallas_call(
        functools.partial(gram_kernel, groups, len(own)),
        out_shape=shapes,
        in_specs=[pl.BlockSpec(memory_space=pl.ANY)] * len(inputs),
        out_specs=[pl.BlockSpec(memory_space=pl.ANY)] * len(shapes),
        scratch_shapes=[pltpu.VMEM(shape.shape, shape.dtype) for shape in shapes]
        + [pltpu.VMEM((TAIL, BLOCK), F32)] * len(groups)
        + [
            pltpu.VMEM((rows, BLOCK, 2 * GROUP), BF16),
            pltpu.SemaphoreType.DMA,
            pltpu.SemaphoreType.DMA((len(shapes),)),
        ],
        compiler_params=pltpu.CompilerParams(vmem_limit_bytes=GRAM_VMEM),
        cost_estimate=pl.CostEstimate(
            flops=len(own) // 2 * MINE * 2 * BLOCK * BLOCK * 2 * GROUP,
            bytes_accessed=rows << 16,
            transcendentals=0,
        ),
        name="gram",
    )(*inputs)


def add_call(groups, stage, inputs, early):
    if stage < 2:
        shapes = [shape for group in groups for shape in exchange_shapes(group, stage + 1)]
        scratch = [pltpu.VMEM((TAIL, BLOCK), F32)] * len(groups)
        early = []
    else:
        extra = 1 if early else 0
        shapes = [
            jax.ShapeDtypeStruct((len(blocks[0]) + extra, UNIT, BLOCK), BF16) for blocks, _ in groups
        ]
        scratch = []
    inputs = inputs + early
    return pl.pallas_call(
        functools.partial(add_kernel, groups, stage, len(early)),
        out_shape=shapes,
        in_specs=[pl.BlockSpec(memory_space=pltpu.VMEM)] * len(inputs),
        out_specs=[pl.BlockSpec(memory_space=pltpu.VMEM)] * len(shapes),
        scratch_shapes=scratch,
        compiler_params=pltpu.CompilerParams(vmem_limit_bytes=40 << 20),
        cost_estimate=pl.CostEstimate(flops=1 << 16, bytes_accessed=1 << 16, transcendentals=0),
        name="add",
    )(*inputs)


def summed(groups, parts, stage, early=(), beside=None):
    inputs = []
    for g, (_, order) in enumerate(groups):
        inputs += [parts[2 * g], MOVES[order[stage]](parts[2 * g + 1])]
    if beside is not None:
        inputs, beside = lax.optimization_barrier((inputs, beside))
        return add_call(groups, stage, inputs, list(early)), beside
    return add_call(groups, stage, inputs, list(early))


def gathered(mine):
    thirds = range(3)

    def move(stage, pieces):
        return [
            ([by ^ ORDERS[t][stage] for by in pieces[t][0]], MOVES[ORDERS[t][stage]](pieces[t][1]))
            for t in thirds
        ]

    def wave(*groups):
        return lax.optimization_barrier(groups)

    out = []

    def place_in(pieces, core):
        out.extend(((t, bys, core), piece) for t, (bys, piece) in enumerate(pieces))

    def across(pieces):
        place_in(pieces, 0)
        place_in([(bys, over_core(piece)) for bys, piece in pieces], 1)

    def merge(a, b):
        return [(p[0] + q[0], jnp.concatenate([p[1], q[1]])) for p, q in zip(a, b)]

    def unkeyed(pieces):
        return [piece for _, piece in pieces]

    def keyed(pieces, arrays):
        return [(bys, array) for (bys, _), array in zip(pieces, arrays)]

    def ordered(*groups):
        done = wave([unkeyed(group) for group in groups], [piece for _, piece in out[:-6]])
        out[:-6] = [(key, piece) for (key, _), piece in zip(out, done[1])]
        return [keyed(group, arrays) for group, arrays in zip(groups, done[0])]

    own = [([0], piece) for piece in mine]
    pair = merge(own, move(0, own))
    second = move(1, pair)
    across(pair)
    pair, second = ordered(pair, second)
    third_a = move(2, pair)
    across(second)
    second, third_a = ordered(second, third_a)
    third_b = move(2, second)
    across(third_a)
    across(third_b)
    return out


def step_kernel(keys, part, *refs):
    gram_pieces = refs[: len(keys)]
    refs = refs[len(keys) :]
    iter_pieces = refs[: len(PIECES)]
    outs = refs[len(PIECES) : len(PIECES) + 4]
    gram, panel, first, total, result, here, there, gone = refs[len(PIECES) + 4 :]
    y, x, core, high, low = place()
    for p in range(len(PIECES)):
        for step in range(4):
            pltpu.make_async_copy(
                iter_pieces[p].at[step, :, :, pl.ds(part * WIDE, WIDE)],
                panel.at[block_rows(p), slab_of(high, low, step)],
                there,
            ).start()
    for (third, bys, other), piece in zip(keys, gram_pieces):
        lo, hi = THIRDS[third]
        for n, by in enumerate(bys):
            pltpu.make_async_copy(
                piece.at[n],
                gram.at[
                    pl.ds(flip(core, other) * MINE + lo, hi - lo), place_of(x, y, low, by)
                ],
                here,
            ).start()
    pltpu.make_async_copy(panel, panel, there).wait()
    pltpu.make_async_copy(gram, gram, here).wait()

    def rows_of(i):
        return pl.ds(pl.multiple_of(i * BLOCK, BLOCK), BLOCK)

    def block(d, i):
        return gram[lookup(i, [SPOT[n, d] for n in range(BLOCKS)])].reshape(BLOCK, BLOCK)

    def apply(source, i):
        got = dot(block(0, i), source(i), ((1,), (0,)))
        for d in range(1, DIAGS):
            j = lax.rem(i + d, BLOCKS)
            got += dot(block(d, i), source(j), ((1,), (0,)))
            j = lax.rem(i + BLOCKS - d, BLOCKS)
            got += dot(block(d, j), source(j), ((0,), (0,)))
        return got

    def iter_rows(i):
        return panel[i].reshape(BLOCK, WIDE)

    def one(i, carry):
        got = apply(iter_rows, i)
        first[rows_of(i), :] = got.astype(BF16)
        total[rows_of(i), :] = quint_a * iter_rows(i).astype(F32) + quint_b * got
        return carry

    def two(i, carry):
        got = apply(lambda j: first[rows_of(j), :], i)
        result[i] = (total[rows_of(i), :] + quint_c * got).astype(BF16).reshape(4, BAND, WIDE)
        for step in range(4):
            pltpu.make_async_copy(
                result.at[i, slab_of(y, low, step)], outs[step].at[i], gone.at[step]
            ).start()
        return carry

    lax.fori_loop(0, BLOCKS, one, 0)
    lax.fori_loop(0, BLOCKS, two, 0)
    for step in range(4):
        pltpu.make_async_copy(result.at[:, 0], outs[step], gone.at[step]).wait()


def step_call(keys, gram_pieces, iter_pieces, part):
    count = len(gram_pieces) + len(iter_pieces)
    return pl.pallas_call(
        functools.partial(step_kernel, keys, part),
        out_shape=[jax.ShapeDtypeStruct((BLOCKS, BAND, WIDE), BF16)] * 4,
        in_specs=[pl.BlockSpec(memory_space=pl.ANY)] * count,
        out_specs=[pl.BlockSpec(memory_space=pl.ANY)] * 4,
        scratch_shapes=[
            pltpu.VMEM((2 * MINE, PLACES, UNIT, BLOCK), BF16),
            pltpu.VMEM((BLOCKS, 4, BAND, WIDE), BF16),
            pltpu.VMEM((ORDER, WIDE), BF16),
            pltpu.VMEM((ORDER, WIDE), F32),
            pltpu.VMEM((BLOCKS, 4, BAND, WIDE), BF16),
            pltpu.SemaphoreType.DMA,
            pltpu.SemaphoreType.DMA,
            pltpu.SemaphoreType.DMA((4,)),
        ],
        compiler_params=pltpu.CompilerParams(vmem_limit_bytes=STEP_VMEM),
        cost_estimate=pl.CostEstimate(
            flops=4 * ORDER * ORDER * WIDE, bytes_accessed=20 << 20, transcendentals=0
        ),
        name="step",
    )(*gram_pieces, *iter_pieces)


def pick(a, at, size, axis):
    return lax.dynamic_slice_in_dim(a, at, size, axis)


def panels(iterate):
    y, x, core, high, low = place()
    aligned = y == high
    starts = [sum(HOPS[:n]) * BAND for n in range(len(HOPS))]

    def cast(n, at):
        size = (HOPS[n] * BAND, 2 * GROUP)
        return lax.dynamic_slice(iterate, (starts[n], at * 2 * GROUP), size).astype(BF16)

    def chunks(keep, other):
        near, far = jnp.where(aligned, keep, other), jnp.where(aligned, other, keep)
        return [
            pick(far if step >> 1 else near, flip(low, step & 1) * GROUP, GROUP, 1)
            for step in range(4)
        ]

    def travel(ready):
        return [ready[0]] + [over_z(ready[step], step) for step in (1, 2, 3)]

    def joined(pieces):
        return jnp.stack([jnp.concatenate(slab) for slab in zip(*pieces)]).reshape(4, -1, BAND, GROUP)

    done = []
    keep, other = cast(0, y), over_y(cast(0, 1 - y))
    ahead = [(cast(n, y), cast(n, 1 - y)) for n in range(1, len(HOPS))]
    for n in range(len(HOPS) - 1):
        ready, ahead = lax.optimization_barrier((chunks(keep, other), ahead))
        done.append(travel(ready))
        keep, other = ahead[n][0], over_y(ahead[n][1])
    ready = chunks(keep, other)
    own = [joined(done)]
    done, parts, start = [], None, 0
    for n, blocks in enumerate(LAST):
        stop = start + blocks * BAND
        now, ready, done, own, parts = lax.optimization_barrier(
            ([chunk[start:stop] for chunk in ready], ready, done, own, parts)
        )
        start = stop
        done.append(travel(now))
        if n == 0:
            beside = [over_core(own[0])]
            parts = gram_call(EARLY_GROUPS, own, beside)
        else:
            parts = summed(EARLY_GROUPS, parts, n - 1)
            own.append(joined(done[:1]))
            beside.append(over_core(own[1]))
    out = (FACTOR * quint_a) * (iterate - lax.reduce_precision(iterate, 8, 7))
    out, parts, done = lax.optimization_barrier((out, parts, done))
    own.append(joined(done[1:]))
    beside.append(over_core(own[2]))
    return own, beside, parts, out


def shards_cube(iterate):
    y, x, core, high, low = place()
    own, beside, early, out = panels(iterate)
    early, mine = summed(EARLY_GROUPS, early, 1, beside=gram_call(LATE_GROUPS, own, beside))
    early = summed(EARLY_GROUPS, early, 2)
    mine, early = lax.optimization_barrier((summed(LATE_GROUPS, mine, 0), early))
    for stage in (1, 2):
        mine = summed(LATE_GROUPS, mine, stage, early)
    entries = gathered([piece[None] for piece in mine])
    keys = [key for key, _ in entries]
    gram_pieces = [piece.reshape(-1, *piece.shape[-3:]) for _, piece in entries]

    before = None
    for part in range(HALVES):
        slabs = step_call(keys, gram_pieces, own, part)
        if before is not None:
            slabs, before = lax.optimization_barrier((slabs, before))
        got = [home(slabs[step], step) for step in range(4)]
        for step in range(4):
            at = slab_of(high, low, step) * GROUP + part * WIDE
            piece = FACTOR * got[step].reshape(SLAB, WIDE).astype(F32)
            out = lax.dynamic_update_slice_in_dim(out, pick(out, at, WIDE, 1) + piece, at, 1)
        before = got
    return out


def solution(mesh):
    shards = shards_cube if dict(mesh.shape) == {"mats": 2, "col": 4, "row": 4} else shards_rows
    in_specs = (P(("mats", "row"), "col"),)
    out_specs = P(("mats", "row"), "col")
    return jax.shard_map(shards, mesh=mesh, in_specs=in_specs, out_specs=out_specs, check_vma=False)
```
